32 devices in a mesh: ctx: 8 (over z, y), tp: 4 (over x, core).
Axes of the slice: x: 2, y: 2, z: 4, core: 2. Of those that a mesh axis runs over, the one named last changes fastest.
Arguments:
- queries: bfloat16 [1024, 5120], P('ctx', 'tp'), may hold values from -40 to 40
- keys: bfloat16 [1024, 1024], P('ctx', 'tp'), may hold values from -40 to 40
- values: bfloat16 [1024, 1024], P('ctx', 'tp'), may hold values from -6 to 6
- out_grad: bfloat16 [1024, 5120], P('ctx', 'tp'), may hold values from -6 to 6
- ancestry: int32 [8, 5], replicated, may hold values from 0 to 7, as said below
- w_query: bfloat16 [5120, 5120], P(None, 'tp'), may hold values from -0.078125 to 0.078125
- key_matrix: bfloat16 [5120, 1024], P(None, 'tp'), may hold values from -0.078125 to 0.078125
- value_matrix: bfloat16 [5120, 1024], P(None, 'tp'), may hold values from -0.078125 to 0.078125
Outputs:
- input_grad: bfloat16 [1024, 5120], P('ctx', 'tp')
The draws below stay inside these ranges and needn't reach their ends.
Inputs may be any that keep to these rules, and one draw needn't show every extreme that they name: `ancestry`: row b holds b, then its ancestors in order parent, grandparent and so on (each an earlier block), then b again to fill the row. Blocks 0 to 4 form one chain, each the parent of the next; no block has more than 4 ancestors; every block descends from blocks 0 to 0 or is one of them.
All inputs are finite; a program needn't handle non-finite values.
Results may differ from the reference program's by a relative error of at most 0.024.
Values may be sent and summed in bfloat16 or wider, within the bound.
A program may use at most 128 MiB of HBM per device.

```python
import math
import jax
import jax.numpy as jnp
from jax import lax

MODEL_WIDTH = 5120
QUERY_HEADS = 40
KEY_VALUE_HEADS = 8
HEAD_SIZE = 128
TREE_BLOCK_SIZE = 128
PACK_TOKENS = 1024
PACK_BLOCKS = 8
PROMPT_BLK = 1
DEPTH = 4
ANC = 5


def draw_keys(key, part):
    random_jitter = jax.random.truncated_normal(jax.random.fold_in(key, 1), -4.0, 4.0, (PACK_TOKENS, KEY_VALUE_HEADS * HEAD_SIZE), jnp.float32)
    return random_jitter.astype(jnp.bfloat16)


def draw_queries(key, part):
    random_jitter = jax.random.truncated_normal(jax.random.fold_in(key, 3), -4.0, 4.0, (PACK_TOKENS, QUERY_HEADS * HEAD_SIZE), jnp.float32)
    return random_jitter.astype(jnp.bfloat16)


def draw_ancestry(key, part):
    base_key = jax.random.fold_in(key, 99)
    coin_key, pick_key = jax.random.split(base_key)
    coin_flips = jax.random.randint(coin_key, (PACK_BLOCKS,), 0, 2)
    pick_draws = jax.random.randint(pick_key, (PACK_BLOCKS,), 0, 1 << 20)
    lowest = PROMPT_BLK - 1

    def place(carry, block_id):
        depths, parents = carry
        previous = jnp.maximum(block_id - 1, 0)
        spread = jnp.maximum(block_id - lowest, 1)
        candidate = lowest + pick_draws[block_id] % spread
        candidate = jnp.where(depths[candidate] < DEPTH, candidate, lowest)
        extend = (coin_flips[block_id] == 1) & (depths[previous] < DEPTH)
        fallback = jnp.where(extend, previous, candidate)
        parent = jnp.where(block_id <= DEPTH, previous, fallback)
        block_depth = jnp.where(block_id == 0, 0, depths[parent] + 1)
        return ((depths.at[block_id].set(block_depth), parents.at[block_id].set(parent)), 0)
    start_carry = (jnp.zeros((PACK_BLOCKS,), jnp.int32), jnp.zeros((PACK_BLOCKS,), jnp.int32))
    (depths, parents), unused = lax.scan(place, start_carry, jnp.arange(PACK_BLOCKS, dtype=jnp.int32))
    own_ids = jnp.arange(PACK_BLOCKS, dtype=jnp.int32)
    walker = own_ids
    columns = [own_ids]
    for step_id in range(1, ANC):
        walker = parents[walker]
        columns.append(jnp.where(step_id <= depths, walker, own_ids))
    return jnp.stack(columns, axis=1)


def steps_of(key, dims, shards, low, largest):
    gain = 1.0
    for dim, shards_of in shards:
        draws = jax.random.uniform(jax.random.fold_in(jax.random.fold_in(key, 6), dim), (shards_of,), jnp.float32, low / len(shards), largest / len(shards))
        gain = gain * jnp.repeat(jnp.exp(draws), dims[dim] // shards_of).reshape((-1,) + (1,) * (len(dims) - 1 - dim))
    return gain


def scatter_about(stream_key, dims, scale, bound, cuts=(), kind=jnp.bfloat16):
    loudness = steps_of(stream_key, dims, cuts, -0.22, 0.18) if cuts else 1.0
    entries = jax.random.normal(stream_key, dims, jnp.float32) * scale * loudness
    return jnp.minimum(jnp.maximum(entries, -bound), bound).astype(kind)


def setup_inputs(seed: int = 0) -> dict:
    arg_keys = jax.random.split(jax.random.key(seed), 9)
    return {
        "queries": draw_queries(jax.random.fold_in(arg_keys[8], 71), 0),
        "keys": draw_keys(jax.random.fold_in(arg_keys[8], 71), 0),
        "values": scatter_about(arg_keys[2], (PACK_TOKENS, KEY_VALUE_HEADS * HEAD_SIZE), 1.0, 6.0, ((0, 8), (1, 4))),
        "out_grad": scatter_about(arg_keys[3], (PACK_TOKENS, QUERY_HEADS * HEAD_SIZE), 1.0, 6.0, ((0, 8), (1, 4))),
        "ancestry": draw_ancestry(jax.random.fold_in(arg_keys[8], 71), 0),
        "w_query": scatter_about(arg_keys[5], (MODEL_WIDTH, QUERY_HEADS * HEAD_SIZE), MODEL_WIDTH ** -0.5, 0.078125, ((1, 4),)),
        "key_matrix": scatter_about(arg_keys[6], (MODEL_WIDTH, KEY_VALUE_HEADS * HEAD_SIZE), MODEL_WIDTH ** -0.5, 0.078125, ((1, 4),)),
        "value_matrix": scatter_about(arg_keys[7], (MODEL_WIDTH, KEY_VALUE_HEADS * HEAD_SIZE), MODEL_WIDTH ** -0.5, 0.078125, ((1, 4),)),
    }


ROPE_BASE = 1000000.0
MASKED = -1.0e30


def inverse_rotary(grads, token_places):
    half_width = grads.shape[-1] // 2
    frequencies = jnp.exp(jnp.arange(half_width, dtype=jnp.float32) * (-2.0 * math.log(ROPE_BASE) / grads.shape[-1]))
    angles = token_places[:, None] * frequencies[None, :]
    cosine = jnp.cos(angles)[:, None, :]
    sine_part = jnp.sin(angles)[:, None, :]
    front_half = grads[..., :half_width]
    second = grads[..., half_width:]
    return jnp.concatenate([front_half * cosine + second * sine_part, second * cosine - front_half * sine_part], axis=-1)


def reference(queries, keys, values, out_grad, ancestry, w_query, key_matrix, value_matrix):
    heads_per_group = QUERY_HEADS // KEY_VALUE_HEADS
    factor = HEAD_SIZE ** -0.5
    every_block = jnp.arange(PACK_BLOCKS, dtype=jnp.int32)
    depths = jnp.sum((ancestry != every_block[:, None]).astype(jnp.int32), axis=1)
    token_ids = jnp.arange(PACK_TOKENS, dtype=jnp.int32)
    token_block = token_ids // TREE_BLOCK_SIZE
    listed = jnp.any(ancestry[:, :, None] == every_block[None, None, :], axis=1)
    visible = listed[token_block][:, token_block] & ((token_block[:, None] != token_block[None, :]) | (token_ids[None, :] <= token_ids[:, None]))
    token_places = (TREE_BLOCK_SIZE * depths[token_block] + token_ids % TREE_BLOCK_SIZE).astype(jnp.float32)
    query_heads = queries.reshape(PACK_TOKENS, QUERY_HEADS, HEAD_SIZE).transpose(1, 0, 2)
    grad_heads = out_grad.reshape(PACK_TOKENS, QUERY_HEADS, HEAD_SIZE).transpose(1, 0, 2)
    heads_of_key = keys.reshape(PACK_TOKENS, KEY_VALUE_HEADS, HEAD_SIZE).transpose(1, 0, 2)
    heads_of_value = values.reshape(PACK_TOKENS, KEY_VALUE_HEADS, HEAD_SIZE).transpose(1, 0, 2)

    def one_head(inputs):
        query_h, grad_h, kv_index = inputs
        key_h = heads_of_key[kv_index]
        value_h = heads_of_value[kv_index]
        scores = jnp.dot(query_h, key_h.T, preferred_element_type=jnp.float32) * factor
        scores = jnp.where(visible, scores, MASKED)
        maxima = jnp.max(scores, axis=1)
        weights = jnp.where(visible, jnp.exp(scores - maxima[:, None]), 0.0)
        totals = jnp.sum(weights, axis=1)
        attended = (jnp.dot(weights.astype(jnp.bfloat16), value_h, preferred_element_type=jnp.float32) / totals[:, None]).astype(jnp.bfloat16)
        log_totals = maxima + jnp.log(totals)
        row_dots = jnp.sum(grad_h.astype(jnp.float32) * attended.astype(jnp.float32), axis=1)
        probs = jnp.where(visible, jnp.exp(scores - log_totals[:, None]), 0.0)
        prob_grads = jnp.dot(grad_h, value_h.T, preferred_element_type=jnp.float32)
        score_grads = (probs * (prob_grads - row_dots[:, None])).astype(jnp.bfloat16)
        query_grad = jnp.dot(score_grads, key_h, preferred_element_type=jnp.float32) * factor
        key_grad = jnp.dot(score_grads.T, query_h, preferred_element_type=jnp.float32) * factor
        value_grad = jnp.dot(probs.astype(jnp.bfloat16).T, grad_h, preferred_element_type=jnp.float32)
        return query_grad, key_grad, value_grad

    kv_of_head = jnp.arange(QUERY_HEADS, dtype=jnp.int32) // heads_per_group
    query_grads, gradient_keys, gradient_values = lax.map(one_head, (query_heads, grad_heads, kv_of_head))
    query_low = inverse_rotary(query_grads.transpose(1, 0, 2), token_places).astype(jnp.bfloat16).reshape(PACK_TOKENS, QUERY_HEADS * HEAD_SIZE)
    summed_key = gradient_keys.reshape(KEY_VALUE_HEADS, heads_per_group, PACK_TOKENS, HEAD_SIZE).sum(axis=1).transpose(1, 0, 2)
    summed_value = gradient_values.reshape(KEY_VALUE_HEADS, heads_per_group, PACK_TOKENS, HEAD_SIZE).sum(axis=1).transpose(1, 0, 2)
    key_reduced = inverse_rotary(summed_key, token_places).astype(jnp.bfloat16).reshape(PACK_TOKENS, KEY_VALUE_HEADS * HEAD_SIZE)
    value_reduced = summed_value.astype(jnp.bfloat16).reshape(PACK_TOKENS, KEY_VALUE_HEADS * HEAD_SIZE)
    summed = jnp.dot(query_low, w_query.T, preferred_element_type=jnp.float32)
    summed = summed + jnp.dot(key_reduced, key_matrix.T, preferred_element_type=jnp.float32)
    summed = summed + jnp.dot(value_reduced, value_matrix.T, preferred_element_type=jnp.float32)
    return summed.astype(jnp.bfloat16)
```

```python
import functools
import math

import jax
import jax.numpy as jnp
from jax import lax
from jax.experimental import pallas as pl
from jax.experimental.pallas import tpu as pltpu
from jax.sharding import PartitionSpec as P

HEAD_SIZE = 128
ROPE_BASE = 1000000.0
MASKED = -1e30
MESH = pl.DeviceIdType.MESH
F32 = jnp.float32
BF16 = jnp.bfloat16
BY_LAST = (((1,), (1,)), ((), ()))
PLAIN = (((1,), (0,)), ((), ()))


def dot(a, b, contract=PLAIN):
    return lax.dot_general(a, b, contract, preferred_element_type=F32)


def kernel(
    nz, ny, nx,
    anc_ref, q_ref, k_ref, v_ref, g_ref, wq_ref, wk_ref, wv_ref, out_ref,
    w_all, kv_all, q_rows, g_rows, s_scr, p_scr, slots, stage, yrecv, zrecv, total,
    x_all, acc, sib_send, sib_recv, x_send, x_recv,
    w_sem, up_sem, side_sem, kv_sem, ys_sem, yr_sem, zs_sem, zr_sem,
    ss_sem, sr_sem, xs_sem, xr_sem,
):
    tok, q_width = q_ref.shape
    kv_width = k_ref.shape[1]
    kv_local = kv_width // HEAD_SIZE
    group = q_width // kv_width
    rows = group * tok
    n_slots = anc_ref.shape[1]
    deepest = n_slots - 1
    factor = HEAD_SIZE ** -0.5
    half_head = HEAD_SIZE // 2
    chunk = acc.shape[2]
    per = out_ref.shape[1] // chunk

    me, t = lax.axis_index("ctx"), lax.axis_index("tp")
    z, y = me // ny, me % ny
    x, core = t // 2, t % 2

    def remote(src, dst, send, recv, ctx, tp):
        return pltpu.make_async_remote_copy(
            src_ref=src, dst_ref=dst, send_sem=send, recv_sem=recv,
            device_id=(ctx, tp), device_id_type=MESH,
        )

    weights = (
        pltpu.make_async_copy(wq_ref, w_all.at[:, pl.ds(0, q_width)], w_sem.at[0]),
        pltpu.make_async_copy(wk_ref, w_all.at[:, pl.ds(q_width, kv_width)], w_sem.at[1]),
        pltpu.make_async_copy(wv_ref, w_all.at[:, pl.ds(q_width + kv_width, kv_width)], w_sem.at[2]),
    )
    for copy in weights:
        copy.start()

    barrier = pltpu.get_barrier_semaphore()

    def greet(ctx, tp):
        pl.semaphore_signal(barrier, inc=1, device_id=(ctx, tp), device_id_type=MESH)

    @pl.when(z > 0)
    def _():
        greet(me - ny, t)

    @pl.when(z < nz - 1)
    def _():
        greet(me + ny, t)

    for dy in range(1, ny):
        greet(z * ny + (y + dy) % ny, t)
    greet(me, x * 2 + 1 - core)
    for dx in range(1, nx):
        greet(me, ((x + dx) % nx) * 2 + core)
    kv_all[me, 0] = k_ref[...]
    kv_all[me, 1] = v_ref[...]
    peers = ny - 1 + nx + (z > 0).astype(jnp.int32) + (z < nz - 1).astype(jnp.int32)
    pl.semaphore_wait(barrier, peers)

    def up_copy(r, half):
        j = r * ny + y
        return remote(
            kv_all.at[j, half], kv_all.at[j, half], up_sem.at[r, half], kv_sem.at[j, half],
            me + ny, t,
        )

    def side_copy(r, yy, half):
        j = r * ny + y
        return remote(
            kv_all.at[j, half], kv_all.at[j, half], side_sem.at[r, yy, half], kv_sem.at[j, half],
            z * ny + yy, t,
        )

    def kv_arrival(j, half):
        remote(
            kv_all.at[j, half], kv_all.at[j, half], up_sem.at[0, half], kv_sem.at[j, half],
            me, t,
        ).wait_recv()

    for k in range(nz):
        r = z - k
        live = (r >= 0) & (r * ny + y != deepest)
        for half in range(2):
            if k > 0:
                @pl.when(live)
                def _():
                    kv_arrival(r * ny + y, half)

            @pl.when(live & (z < nz - 1))
            def _():
                up_copy(r, half).start()

            for dy in range(1, ny):
                yy = (y + dy) % ny

                @pl.when(live & ((k > 0) | (y < yy)))
                def _():
                    side_copy(r, yy, half).start()

        if k == 0:
            for h in range(kv_local):
                for g in range(group):
                    head = (h * group + g) * HEAD_SIZE
                    q_rows[h, g * tok:(g + 1) * tok, :] = q_ref[:, head:head + HEAD_SIZE]
                    g_rows[h, g * tok:(g + 1) * tok, :] = g_ref[:, head:head + HEAD_SIZE]
            depth = jnp.int32(0)
            for s in range(1, n_slots):
                depth += (anc_ref[me, s] != me).astype(jnp.int32)
            start = (depth * tok).astype(F32)
            scale = -2.0 * math.log(ROPE_BASE) / HEAD_SIZE
            which = lax.broadcasted_iota(jnp.int32, (half_head, tok), 0).astype(F32)
            place = lax.broadcasted_iota(jnp.int32, (half_head, tok), 1).astype(F32) + start
            angles = place * jnp.exp(which * scale)
            cos_t, sin_t = jnp.cos(angles), jnp.sin(angles)

    for k in range(nz):
        r = z - k
        for dy in range(1, ny):
            yy = (y + dy) % ny
            for half in range(2):
                @pl.when((r >= 0) & ((k > 0) | (yy < y)) & (r * ny + yy != deepest))
                def _():
                    kv_arrival(r * ny + yy, half)

    slots[n_slots] = jnp.zeros_like(slots[n_slots])
    power = factor * math.log2(math.e)
    key_id = lax.broadcasted_iota(jnp.int32, (tok, rows), 0)
    query_id = lax.broadcasted_iota(jnp.int32, (tok, rows), 1) % tok
    causal = key_id <= query_id
    for h in range(kv_local):
        cols = slice(h * HEAD_SIZE, (h + 1) * HEAD_SIZE)
        queries = q_rows[h]
        grads = g_rows[h]
        highest = jnp.full((1, rows), MASKED, F32)
        for s in range(n_slots):
            block = me if s == 0 else anc_ref[me, s]
            scores = dot(kv_all[block, 0, :, cols], queries, BY_LAST)
            if s == 0:
                scores = jnp.where(causal, scores, MASKED)
            else:
                scores = scores + jnp.where(block != me, 0.0, MASKED)
            s_scr[s] = scores
            highest = jnp.maximum(highest, jnp.max(scores, axis=0, keepdims=True))
            p_scr[s] = dot(kv_all[block, 1, :, cols], grads, BY_LAST)
        sums = jnp.zeros((1, rows), F32)
        dots = jnp.zeros((1, rows), F32)
        for s in range(n_slots):
            weights_s = jnp.exp2((s_scr[s] - highest) * power)
            s_scr[s] = weights_s
            sums = sums + jnp.sum(weights_s, axis=0, keepdims=True)
            dots = dots + jnp.sum(weights_s * p_scr[s], axis=0, keepdims=True)
        inverse = 1.0 / sums
        dots = dots * inverse
        query_grad = jnp.zeros((HEAD_SIZE, rows), F32)
        for s in range(n_slots):
            block = me if s == 0 else anc_ref[me, s]
            probs = s_scr[s] * inverse
            score_grads = (probs * (p_scr[s] - dots)).astype(BF16)
            slots[s, 0, :, cols] = (dot(score_grads, queries) * factor).astype(BF16)
            slots[s, 1, :, cols] = dot(probs.astype(BF16), grads).astype(BF16)
            keys_t = kv_all[block, 0, :, cols].T
            query_grad = query_grad + dot(keys_t, score_grads)
        query_grad = query_grad * factor
        for g in range(group):
            one = query_grad[:, g * tok:(g + 1) * tok]
            a, b = one[:half_head], one[half_head:]
            turned = jnp.concatenate([a * cos_t + b * sin_t, b * cos_t - a * sin_t], axis=0)
            head = (h * group + g) * HEAD_SIZE
            x_all[:, head:head + HEAD_SIZE] = turned.T.astype(BF16)

    def slot_of(j):
        found = jnp.int32(n_slots)
        for s in range(n_slots - 1, 0, -1):
            a = anc_ref[me, s]
            found = jnp.where((a == j) & (a != me), s, found)
        return jnp.where(j == me, 0, found)

    def y_copy(r, yy, half):
        return remote(
            stage.at[r * ny + yy, half], yrecv.at[r, y, half],
            ys_sem.at[r, yy, half], yr_sem.at[r, y, half], z * ny + yy, t,
        )

    def y_arrival(r, yy, half):
        remote(
            stage.at[r * ny + yy, half], yrecv.at[r, yy, half],
            ys_sem.at[r, yy, half], yr_sem.at[r, yy, half], me, t,
        ).wait_recv()

    def z_copy(r, half):
        return remote(
            stage.at[r * ny + y, half], zrecv.at[r, half],
            zs_sem.at[r, half], zr_sem.at[r, half], me - ny, t,
        )

    def y_sends(r, yy):
        return (r <= z) & ((r < z) | (yy < y)) & (r * ny + yy != deepest)

    for r in range(nz):
        for dy in range(1, ny):
            yy = (y + dy) % ny

            @pl.when(y_sends(r, yy))
            def _():
                j = r * ny + yy
                source = slot_of(j)
                for half in range(2):
                    stage[j, half] = slots[source, half]
                    y_copy(r, yy, half).start()

    for copy in weights:
        copy.wait()
    n_chunks = acc.shape[0]

    def query_part(i, carry):
        w = w_all[pl.ds(pl.multiple_of(i * chunk, chunk), chunk), pl.ds(0, q_width)]
        acc[i] = dot(x_all[:, 0:q_width], w, BY_LAST)
        return carry

    for r in range(nz):
        lax.fori_loop(n_chunks * r // nz, n_chunks * (r + 1) // nz, query_part, 0)

        @pl.when(r <= z)
        def _():
            j = r * ny + y
            source = slot_of(j)
            live = j != deepest
            for half in range(2):
                total[half] = slots[source, half].astype(F32)
                for dy in range(1, ny):
                    yy = (y + dy) % ny

                    @pl.when(live & ((r < z) | (y < yy)))
                    def _():
                        y_arrival(r, yy, half)
                        total[half] += yrecv[r, yy, half].astype(F32)

                @pl.when(live & (z < nz - 1))
                def _():
                    z_copy(r, half).wait_recv()
                    total[half] += zrecv[r, half].astype(F32)

                @pl.when(live & (r < z))
                def _():
                    stage[j, half] = total[half].astype(BF16)
                    z_copy(r, half).start()

    both_cos = jnp.concatenate([cos_t, cos_t], axis=0).T
    both_sin = jnp.concatenate([sin_t, -sin_t], axis=0).T
    for h in range(kv_local):
        one = total[0, :, h * HEAD_SIZE:(h + 1) * HEAD_SIZE]
        swapped = jnp.concatenate([one[:, half_head:], one[:, :half_head]], axis=1)
        at = q_width + h * HEAD_SIZE
        x_all[:, at:at + HEAD_SIZE] = (one * both_cos + swapped * both_sin).astype(BF16)
    x_all[:, q_width + kv_width:] = total[1].astype(BF16)

    def piece(target, i):
        at = target * per + i
        w = w_all[pl.ds(pl.multiple_of(at * chunk, chunk), chunk), pl.ds(q_width, 2 * kv_width)]
        return acc[at] + dot(x_all[:, q_width:], w, BY_LAST)

    def sib_copy(tx, i):
        return remote(
            sib_send.at[tx, i], sib_recv.at[tx, i], ss_sem.at[tx, i], sr_sem.at[tx, i],
            me, x * 2 + 1 - core,
        )

    def x_copy(tx, i):
        return remote(
            x_send.at[tx, i], x_recv.at[x, i], xs_sem.at[tx, i], xr_sem.at[x, i],
            me, tx * 2 + core,
        )

    def x_arrival(sx, i):
        remote(
            x_send.at[sx, i], x_recv.at[sx, i], xs_sem.at[sx, i], xr_sem.at[sx, i], me, t
        ).wait_recv()

    def to_sibling(tx):
        def body(i, carry):
            sib_send[tx, i] = piece(tx * 2 + 1 - core, i).astype(BF16)
            sib_copy(tx, i).start()
            return carry

        lax.fori_loop(0, per, body, 0)

    def from_sibling(tx, i):
        part = piece(tx * 2 + core, i)
        sib_copy(tx, i).wait_recv()
        return part + sib_recv[tx, i].astype(F32)

    for dx in range(1, nx):
        tx = (x + dx) % nx
        to_sibling(tx)

        def across(i, carry):
            x_send[tx, i] = from_sibling(tx, i).astype(BF16)
            x_copy(tx, i).start()
            return carry

        lax.fori_loop(0, per, across, 0)
    to_sibling(x)

    def last(i, carry):
        result = from_sibling(x, i)
        for dx in range(1, nx):
            sx = (x + dx) % nx
            x_arrival(sx, i)
            result = result + x_recv[sx, i].astype(F32)
        out_ref[:, pl.ds(pl.multiple_of(i * chunk, chunk), chunk)] = result.astype(BF16)
        return carry

    lax.fori_loop(0, per, last, 0)

    for k in range(nz):
        r = z - k
        live = (r >= 0) & (r * ny + y != deepest)
        for half in range(2):
            @pl.when(live & (z < nz - 1))
            def _():
                up_copy(r, half).wait_send()

            for dy in range(1, ny):
                yy = (y + dy) % ny

                @pl.when(live & ((k > 0) | (y < yy)))
                def _():
                    side_copy(r, yy, half).wait_send()
    for r in range(nz):
        for half in range(2):
            for dy in range(1, ny):
                yy = (y + dy) % ny

                @pl.when(y_sends(r, yy))
                def _():
                    y_copy(r, yy, half).wait_send()

            @pl.when((r < z) & (r * ny + y != deepest))
            def _():
                z_copy(r, half).wait_send()

    def drain(i, carry):
        for tx in range(nx):
            sib_copy(tx, i).wait_send()
        for dx in range(1, nx):
            x_copy((x + dx) % nx, i).wait_send()
        return carry

    lax.fori_loop(0, per, drain, 0)


def shards(nz, ny, nx, queries, keys, values, out_grad, ancestry, w_query, key_matrix, value_matrix):
    n = nz * ny
    tok, q_width = queries.shape
    kv_width = keys.shape[1]
    kv_local = kv_width // HEAD_SIZE
    rows = tok * (q_width // kv_width)
    model = w_query.shape[0]
    wide = model // (2 * nx)
    chunk = 256 if wide % 256 == 0 else 128
    per = wide // chunk
    n_slots = ancestry.shape[1]
    pair = (2, tok, kv_width)
    dma = pltpu.SemaphoreType.DMA
    vmem = pl.BlockSpec(memory_space=pltpu.VMEM)
    hbm = pl.BlockSpec(memory_space=pl.ANY)
    return pl.pallas_call(
        functools.partial(kernel, nz, ny, nx),
        out_shape=jax.ShapeDtypeStruct((tok, wide), BF16),
        in_specs=[pl.BlockSpec(memory_space=pltpu.SMEM), vmem, vmem, vmem, vmem, hbm, hbm, hbm],
        out_specs=vmem,
        scratch_shapes=[
            pltpu.VMEM((model, q_width + 2 * kv_width), BF16),
            pltpu.VMEM((n,) + pair, BF16),
            pltpu.VMEM((kv_local, rows, HEAD_SIZE), BF16),
            pltpu.VMEM((kv_local, rows, HEAD_SIZE), BF16),
            pltpu.VMEM((n_slots, tok, rows), F32),
            pltpu.VMEM((n_slots, tok, rows), F32),
            pltpu.VMEM((n_slots + 1,) + pair, BF16),
            pltpu.VMEM((n,) + pair, BF16),
            pltpu.VMEM((nz, ny) + pair, BF16),
            pltpu.VMEM((nz,) + pair, BF16),
            pltpu.VMEM(pair, F32),
            pltpu.VMEM((tok, q_width + 2 * kv_width), BF16),
            pltpu.VMEM((model // chunk, tok, chunk), F32),
            pltpu.VMEM((nx, per, tok, chunk), BF16),
            pltpu.VMEM((nx, per, tok, chunk), BF16),
            pltpu.VMEM((nx, per, tok, chunk), BF16),
            pltpu.VMEM((nx, per, tok, chunk), BF16),
            dma((3,)), dma((nz, 2)), dma((nz, ny, 2)), dma((n, 2)),
            dma((nz, ny, 2)), dma((nz, ny, 2)), dma((nz, 2)), dma((nz, 2)),
            dma((nx, per)), dma((nx, per)), dma((nx, per)), dma((nx, per)),
        ],
        compiler_params=pltpu.CompilerParams(
            collective_id=0, has_side_effects=True, vmem_limit_bytes=60 * 1024 * 1024
        ),
        name="tree_attention_backward",
    )(ancestry, queries, keys, values, out_grad, w_query, key_matrix, value_matrix)


def solution(mesh):
    n = mesh.shape["ctx"]
    ny = 2 ** ((n.bit_length() - 1) // 2)
    nx = mesh.shape["tp"] // 2
    in_specs = (
        P("ctx", "tp"),
        P("ctx", "tp"),
        P("ctx", "tp"),
        P("ctx", "tp"),
        P(),
        P(None, "tp"),
        P(None, "tp"),
        P(None, "tp"),
    )
    return jax.shard_map(
        functools.partial(shards, n // ny, ny, nx),
        mesh=mesh, in_specs=in_specs, out_specs=P("ctx", "tp"), check_vma=False,
    )
```

```python
import functools
import math

import jax
import jax.numpy as jnp
from jax import lax
from jax.experimental import pallas as pl
from jax.experimental.pallas import tpu as pltpu
from jax.sharding import PartitionSpec as P

HEAD_SIZE = 128
ROPE_BASE = 1000000.0
MASKED = -1e30
MESH = pl.DeviceIdType.MESH
F32 = jnp.float32
BF16 = jnp.bfloat16
BY_LAST = (((1,), (1,)), ((), ()))
PLAIN = (((1,), (0,)), ((), ()))


def dot(a, b, contract=PLAIN):
    return lax.dot_general(a, b, contract, preferred_element_type=F32)


def kernel(
    nz, ny, nx,
    anc_ref, q_ref, k_ref, v_ref, g_ref, wq_ref, wk_ref, wv_ref, out_ref,
    w_all, kv_all, q_rows, g_rows, s_scr, p_scr, stats, finals, turns, dq_acc, stage, yrecv, zrecv, total,
    x_all, acc, sib_send, sib_recv, x_send, x_recv,
    w_sem, up_sem, side_sem, kv_sem, ys_sem, yr_sem, zs_sem, zr_sem,
    ss_sem, sr_sem, xs_sem, xr_sem,
):
    tok, q_width = q_ref.shape
    kv_width = k_ref.shape[1]
    kv_local = kv_width // HEAD_SIZE
    group = q_width // kv_width
    rows = group * tok
    n_slots = anc_ref.shape[1]
    deepest = n_slots - 1
    factor = HEAD_SIZE ** -0.5
    half_head = HEAD_SIZE // 2
    chunk = acc.shape[2]
    per = out_ref.shape[1] // chunk

    me, t = lax.axis_index("ctx"), lax.axis_index("tp")
    z, y = me // ny, me % ny
    x, core = t // 2, t % 2

    def remote(src, dst, send, recv, ctx, tp):
        return pltpu.make_async_remote_copy(
            src_ref=src, dst_ref=dst, send_sem=send, recv_sem=recv,
            device_id=(ctx, tp), device_id_type=MESH,
        )

    weights = (
        pltpu.make_async_copy(wq_ref, w_all.at[:, pl.ds(0, q_width)], w_sem.at[0]),
        pltpu.make_async_copy(wk_ref, w_all.at[:, pl.ds(q_width, kv_width)], w_sem.at[1]),
        pltpu.make_async_copy(wv_ref, w_all.at[:, pl.ds(q_width + kv_width, kv_width)], w_sem.at[2]),
    )
    for copy in weights:
        copy.start()

    barrier = pltpu.get_barrier_semaphore()

    def greet(ctx, tp):
        pl.semaphore_signal(barrier, inc=1, device_id=(ctx, tp), device_id_type=MESH)

    @pl.when(z > 0)
    def _():
        greet(me - ny, t)

    @pl.when(z < nz - 1)
    def _():
        greet(me + ny, t)

    for dy in range(1, ny):
        greet(z * ny + (y + dy) % ny, t)
    greet(me, x * 2 + 1 - core)
    for dx in range(1, nx):
        greet(me, ((x + dx) % nx) * 2 + core)
    kv_all[me, 0] = k_ref[...]
    kv_all[me, 1] = v_ref[...]
    peers = ny - 1 + nx + (z > 0).astype(jnp.int32) + (z < nz - 1).astype(jnp.int32)
    pl.semaphore_wait(barrier, peers)

    def up_copy(r, half):
        j = r * ny + y
        return remote(
            kv_all.at[j, half], kv_all.at[j, half], up_sem.at[r, half], kv_sem.at[j, half],
            me + ny, t,
        )

    def side_copy(r, yy, half):
        j = r * ny + y
        return remote(
            kv_all.at[j, half], kv_all.at[j, half], side_sem.at[r, yy, half], kv_sem.at[j, half],
            z * ny + yy, t,
        )

    def kv_arrival(j, half):
        remote(
            kv_all.at[j, half], kv_all.at[j, half], up_sem.at[0, half], kv_sem.at[j, half],
            me, t,
        ).wait_recv()

    power = factor * math.log2(math.e)
    head_cols = [slice(h * HEAD_SIZE, (h + 1) * HEAD_SIZE) for h in range(kv_local)]

    def forward(j, own):
        for h, cols in enumerate(head_cols):
            scores = dot(kv_all[j, 0, :, cols], q_rows[h], BY_LAST)
            if own:
                key_id = lax.broadcasted_iota(jnp.int32, (tok, rows), 0)
                query_id = lax.broadcasted_iota(jnp.int32, (tok, rows), 1) % tok
                scores = jnp.where(key_id <= query_id, scores, MASKED)
            highest = jnp.max(scores, axis=0, keepdims=True)
            raw = jnp.exp2((scores - highest) * power)
            prob_grads = dot(kv_all[j, 1, :, cols], g_rows[h], BY_LAST)
            s_scr[j, h] = raw
            p_scr[j, h] = prob_grads
            stats[j, h, 0:1] = highest
            stats[j, h, 1:2] = jnp.sum(raw, axis=0, keepdims=True)
            stats[j, h, 2:3] = jnp.sum(raw * prob_grads, axis=0, keepdims=True)

    def start_block(r, half, first):
        @pl.when((r * ny + y != deepest) & (z < nz - 1))
        def _():
            up_copy(r, half).start()

        for dy in range(1, ny):
            yy = (y + dy) % ny
            later = (y < yy) if first else True

            @pl.when((r * ny + y != deepest) & later)
            def _():
                side_copy(r, yy, half).start()

    def from_sides(r):
        for dy in range(1, ny):
            yy = (y + dy) % ny

            @pl.when(((r < z) | (yy < y)) & (r * ny + yy != deepest))
            def _():
                for half in range(2):
                    kv_arrival(r * ny + yy, half)
                forward(r * ny + yy, False)

    for half in range(2):
        start_block(z, half, True)
    for h in range(kv_local):
        for g in range(group):
            head = (h * group + g) * HEAD_SIZE
            q_rows[h, g * tok:(g + 1) * tok, :] = q_ref[:, head:head + HEAD_SIZE]
            g_rows[h, g * tok:(g + 1) * tok, :] = g_ref[:, head:head + HEAD_SIZE]
    depth = jnp.int32(0)
    for s in range(1, n_slots):
        depth += (anc_ref[me, s] != me).astype(jnp.int32)
    start = (depth * tok).astype(F32)
    scale = -2.0 * math.log(ROPE_BASE) / HEAD_SIZE
    which = lax.broadcasted_iota(jnp.int32, (half_head, tok), 0).astype(F32)
    place = lax.broadcasted_iota(jnp.int32, (half_head, tok), 1).astype(F32) + start
    angles = place * jnp.exp(which * scale)
    turns[0], turns[1] = jnp.cos(angles), jnp.sin(angles)
    dq_acc[...] = jnp.zeros_like(dq_acc)
    for j in range(nz * ny):
        stats[j, :, 0:1] = jnp.full((kv_local, 1, rows), MASKED, F32)
        stats[j, :, 1:3] = jnp.zeros((kv_local, 2, rows), F32)
    forward(me, True)

    def gather_step(k, carry):
        r = z - k

        @pl.when(r * ny + y != deepest)
        def _():
            for half in range(2):
                kv_arrival(r * ny + y, half)
                start_block(r, half, False)
            forward(r * ny + y, False)

        from_sides(r + 1)
        return carry

    lax.fori_loop(1, z + 1, gather_step, 0)
    from_sides(jnp.int32(0))

    shifts = []
    for j in range(nz * ny):
        seen = me == j
        for s in range(1, n_slots):
            seen = seen | (anc_ref[me, s] == j)
        shifts.append(jnp.where(seen, 0.0, MASKED))
    for h in range(kv_local):
        highest = jnp.full((1, rows), MASKED, F32)
        for j in range(nz * ny):
            highest = jnp.maximum(highest, stats[j, h, 0:1] + shifts[j])
        sums = jnp.zeros((1, rows), F32)
        dots = jnp.zeros((1, rows), F32)
        for j in range(nz * ny):
            shrink = jnp.exp2((stats[j, h, 0:1] + shifts[j] - highest) * power)
            stats[j, h, 0:1] = shrink
            sums = sums + shrink * stats[j, h, 1:2]
            dots = dots + shrink * stats[j, h, 2:3]
        inverse = 1.0 / sums
        finals[h, 0:1] = inverse
        finals[h, 1:2] = dots * inverse

    def y_copy(r, yy, half):
        return remote(
            stage.at[r * ny + yy, half], yrecv.at[r, y, half],
            ys_sem.at[r, yy, half], yr_sem.at[r, y, half], z * ny + yy, t,
        )

    def y_arrival(r, yy, half):
        remote(
            stage.at[r * ny + yy, half], yrecv.at[r, yy, half],
            ys_sem.at[r, yy, half], yr_sem.at[r, yy, half], me, t,
        ).wait_recv()

    def z_copy(r, half):
        return remote(
            stage.at[r * ny + y, half], zrecv.at[r, half],
            zs_sem.at[r, half], zr_sem.at[r, half], me - ny, t,
        )

    def y_sends(r, yy):
        return (r <= z) & ((r < z) | (yy < y)) & (r * ny + yy != deepest)

    def backward(j):
        for h, cols in enumerate(head_cols):
            probs = s_scr[j, h] * (stats[j, h, 0:1] * finals[h, 0:1])
            score_grads = (probs * (p_scr[j, h] - finals[h, 1:2])).astype(BF16)
            stage[j, 0, :, cols] = (dot(score_grads, q_rows[h]) * factor).astype(BF16)
            stage[j, 1, :, cols] = dot(probs.astype(BF16), g_rows[h]).astype(BF16)
            dq_acc[h] += dot(kv_all[j, 0, :, cols].T, score_grads)

    def chain(r):
        j = r * ny + y
        live = j != deepest
        for half in range(2):
            total[half] = stage[j, half].astype(F32)
            for dy in range(1, ny):
                yy = (y + dy) % ny

                @pl.when(live & ((r < z) | (y < yy)))
                def _():
                    y_arrival(r, yy, half)
                    total[half] += yrecv[r, yy, half].astype(F32)

            @pl.when(live & (z < nz - 1))
            def _():
                z_copy(r, half).wait_recv()
                total[half] += zrecv[r, half].astype(F32)

            @pl.when(live & (r < z))
            def _():
                stage[j, half] = total[half].astype(BF16)
                z_copy(r, half).start()

    def back_step(r, carry):
        for dy in range(1, ny):
            yy = (y + dy) % ny

            @pl.when(y_sends(r, yy))
            def _():
                backward(r * ny + yy)
                for half in range(2):
                    y_copy(r, yy, half).start()

        @pl.when((r * ny + y != deepest) | (r == z))
        def _():
            backward(r * ny + y)

        @pl.when((z == nz - 1) & (r > 0) & ((r - 1) * ny + y != deepest))
        def _():
            chain(r - 1)

        return carry

    lax.fori_loop(0, z + 1, back_step, 0)
    cos_t, sin_t = turns[0], turns[1]
    for h in range(kv_local):
        query_grad = dq_acc[h] * factor
        for g in range(group):
            one = query_grad[:, g * tok:(g + 1) * tok]
            a, b = one[:half_head], one[half_head:]
            turned = jnp.concatenate([a * cos_t + b * sin_t, b * cos_t - a * sin_t], axis=0)
            head = (h * group + g) * HEAD_SIZE
            x_all[:, head:head + HEAD_SIZE] = turned.T.astype(BF16)

    for copy in weights:
        copy.wait()
    n_chunks = acc.shape[0]

    def query_part(i, carry):
        w = w_all[pl.ds(pl.multiple_of(i * chunk, chunk), chunk), pl.ds(0, q_width)]
        acc[i] = dot(x_all[:, 0:q_width], w, BY_LAST)
        return carry

    first_left = jnp.where(z == nz - 1, z, 0)

    def chain_step(r, carry):
        count = z + 1 - first_left
        at = r - first_left
        lax.fori_loop(n_chunks * at // count, n_chunks * (at + 1) // count, query_part, 0)

        @pl.when((r * ny + y != deepest) | (r == z))
        def _():
            chain(r)

        return carry

    lax.fori_loop(first_left, z + 1, chain_step, 0)

    both_cos = jnp.concatenate([cos_t, cos_t], axis=0).T
    both_sin = jnp.concatenate([sin_t, -sin_t], axis=0).T
    for h in range(kv_local):
        one = total[0, :, h * HEAD_SIZE:(h + 1) * HEAD_SIZE]
        swapped = jnp.concatenate([one[:, half_head:], one[:, :half_head]], axis=1)
        at = q_width + h * HEAD_SIZE
        x_all[:, at:at + HEAD_SIZE] = (one * both_cos + swapped * both_sin).astype(BF16)
    x_all[:, q_width + kv_width:] = total[1].astype(BF16)

    def piece(target, i):
        at = target * per + i
        w = w_all[pl.ds(pl.multiple_of(at * chunk, chunk), chunk), pl.ds(q_width, 2 * kv_width)]
        return acc[at] + dot(x_all[:, q_width:], w, BY_LAST)

    def sib_copy(tx, i):
        return remote(
            sib_send.at[tx, i], sib_recv.at[tx, i], ss_sem.at[tx, i], sr_sem.at[tx, i],
            me, x * 2 + 1 - core,
        )

    def x_copy(tx, i):
        return remote(
            x_send.at[tx, i], x_recv.at[x, i], xs_sem.at[tx, i], xr_sem.at[x, i],
            me, tx * 2 + core,
        )

    def x_arrival(sx, i):
        remote(
            x_send.at[sx, i], x_recv.at[sx, i], xs_sem.at[sx, i], xr_sem.at[sx, i], me, t
        ).wait_recv()

    def to_sibling(tx):
        def body(i, carry):
            sib_send[tx, i] = piece(tx * 2 + 1 - core, i).astype(BF16)
            sib_copy(tx, i).start()
            return carry

        lax.fori_loop(0, per, body, 0)

    def from_sibling(tx, i):
        part = piece(tx * 2 + core, i)
        sib_copy(tx, i).wait_recv()
        return part + sib_recv[tx, i].astype(F32)

    for dx in range(1, nx):
        tx = (x + dx) % nx
        to_sibling(tx)

        def across(i, carry):
            x_send[tx, i] = from_sibling(tx, i).astype(BF16)
            x_copy(tx, i).start()
            return carry

        lax.fori_loop(0, per, across, 0)
    to_sibling(x)

    def last(i, carry):
        result = from_sibling(x, i)
        for dx in range(1, nx):
            sx = (x + dx) % nx
            x_arrival(sx, i)
            result = result + x_recv[sx, i].astype(F32)
        out_ref[:, pl.ds(pl.multiple_of(i * chunk, chunk), chunk)] = result.astype(BF16)
        return carry

    lax.fori_loop(0, per, last, 0)

    for k in range(nz):
        r = z - k
        live = (r >= 0) & (r * ny + y != deepest)
        for half in range(2):
            @pl.when(live & (z < nz - 1))
            def _():
                up_copy(r, half).wait_send()

            for dy in range(1, ny):
                yy = (y + dy) % ny

                @pl.when(live & ((k > 0) | (y < yy)))
                def _():
                    side_copy(r, yy, half).wait_send()
    for r in range(nz):
        for half in range(2):
            for dy in range(1, ny):
                yy = (y + dy) % ny

                @pl.when(y_sends(r, yy))
                def _():
                    y_copy(r, yy, half).wait_send()

            @pl.when((r < z) & (r * ny + y != deepest))
            def _():
                z_copy(r, half).wait_send()

    def drain(i, carry):
        for tx in range(nx):
            sib_copy(tx, i).wait_send()
        for dx in range(1, nx):
            x_copy((x + dx) % nx, i).wait_send()
        return carry

    lax.fori_loop(0, per, drain, 0)


def shards(nz, ny, nx, queries, keys, values, out_grad, ancestry, w_query, key_matrix, value_matrix):
    n = nz * ny
    tok, q_width = queries.shape
    kv_width = keys.shape[1]
    kv_local = kv_width // HEAD_SIZE
    rows = tok * (q_width // kv_width)
    model = w_query.shape[0]
    wide = model // (2 * nx)
    chunk = 256 if wide % 256 == 0 else 128
    per = wide // chunk
    pair = (2, tok, kv_width)
    dma = pltpu.SemaphoreType.DMA
    vmem = pl.BlockSpec(memory_space=pltpu.VMEM)
    hbm = pl.BlockSpec(memory_space=pl.ANY)
    return pl.pallas_call(
        functools.partial(kernel, nz, ny, nx),
        out_shape=jax.ShapeDtypeStruct((tok, wide), BF16),
        in_specs=[pl.BlockSpec(memory_space=pltpu.SMEM), vmem, vmem, vmem, vmem, hbm, hbm, hbm],
        out_specs=vmem,
        scratch_shapes=[
            pltpu.VMEM((model, q_width + 2 * kv_width), BF16),
            pltpu.VMEM((n,) + pair, BF16),
            pltpu.VMEM((kv_local, rows, HEAD_SIZE), BF16),
            pltpu.VMEM((kv_local, rows, HEAD_SIZE), BF16),
            pltpu.VMEM((n, kv_local, tok, rows), F32),
            pltpu.VMEM((n, kv_local, tok, rows), F32),
            pltpu.VMEM((n, kv_local, 8, rows), F32),
            pltpu.VMEM((kv_local, 8, rows), F32),
            pltpu.VMEM((2, HEAD_SIZE // 2, tok), F32),
            pltpu.VMEM((kv_local, HEAD_SIZE, rows), F32),
            pltpu.VMEM((n,) + pair, BF16),
            pltpu.VMEM((nz, ny) + pair, BF16),
            pltpu.VMEM((nz,) + pair, BF16),
            pltpu.VMEM(pair, F32),
            pltpu.VMEM((tok, q_width + 2 * kv_width), BF16),
            pltpu.VMEM((model // chunk, tok, chunk), F32),
            pltpu.VMEM((nx, per, tok, chunk), BF16),
            pltpu.VMEM((nx, per, tok, chunk), BF16),
            pltpu.VMEM((nx, per, tok, chunk), BF16),
            pltpu.VMEM((nx, per, tok, chunk), BF16),
            dma((3,)), dma((nz, 2)), dma((nz, ny, 2)), dma((n, 2)),
            dma((nz, ny, 2)), dma((nz, ny, 2)), dma((nz, 2)), dma((nz, 2)),
            dma((nx, per)), dma((nx, per)), dma((nx, per)), dma((nx, per)),
        ],
        compiler_params=pltpu.CompilerParams(
            collective_id=0, has_side_effects=True, vmem_limit_bytes=60 * 1024 * 1024
        ),
        name="tree_attention_backward",
    )(ancestry, queries, keys, values, out_grad, w_query, key_matrix, value_matrix)


def solution(mesh):
    n = mesh.shape["ctx"]
    ny = 2 ** ((n.bit_length() - 1) // 2)
    nx = mesh.shape["tp"] // 2
    in_specs = (
        P("ctx", "tp"),
        P("ctx", "tp"),
        P("ctx", "tp"),
        P("ctx", "tp"),
        P(),
        P(None, "tp"),
        P(None, "tp"),
        P(None, "tp"),
    )
    return jax.shard_map(
        functools.partial(shards, n // ny, ny, nx),
        mesh=mesh, in_specs=in_specs, out_specs=P("ctx", "tp"), check_vma=False,
    )
```

```python
import functools
import math

import jax
import jax.numpy as jnp
from jax import lax
from jax.experimental import pallas as pl
from jax.experimental.pallas import tpu as pltpu
from jax.sharding import PartitionSpec as P

HEAD_SIZE = 128
ROPE_BASE = 1000000.0
MASKED = -1e30
MESH = pl.DeviceIdType.MESH
F32 = jnp.float32
BF16 = jnp.bfloat16
BY_LAST = (((1,), (1,)), ((), ()))
PLAIN = (((1,), (0,)), ((), ()))


def dot(a, b, contract=PLAIN):
    return lax.dot_general(a, b, contract, preferred_element_type=F32)


def kernel(
    nz, ny, nx,
    anc_ref, q_ref, k_ref, v_ref, g_ref, wq_ref, wk_ref, wv_ref, out_ref,
    w_all, kv_all, q_rows, g_rows, s_scr, p_scr, stats, finals, turns, dq_acc, stage, yrecv, zrecv, total,
    x_all, acc, sib_send, sib_recv, x_send, x_recv,
    w_sem, row_sem, up_sem, side_sem, kv_sem, ys_sem, yr_sem, zs_sem, zr_sem,
    ss_sem, sr_sem, xs_sem, xr_sem,
):
    tok, q_width = q_ref.shape
    kv_width = k_ref.shape[1]
    kv_local = kv_width // HEAD_SIZE
    group = q_width // kv_width
    rows = group * tok
    n_slots = anc_ref.shape[1]
    deepest = n_slots - 1
    factor = HEAD_SIZE ** -0.5
    half_head = HEAD_SIZE // 2
    chunk = acc.shape[2]
    per = out_ref.shape[1] // chunk

    me, t = lax.axis_index("ctx"), lax.axis_index("tp")
    z, y = me // ny, me % ny
    x, core = t // 2, t % 2

    def remote(src, dst, send, recv, ctx, tp):
        return pltpu.make_async_remote_copy(
            src_ref=src, dst_ref=dst, send_sem=send, recv_sem=recv,
            device_id=(ctx, tp), device_id_type=MESH,
        )

    weights = (
        pltpu.make_async_copy(wq_ref, w_all.at[:, pl.ds(0, q_width)], w_sem.at[0]),
        pltpu.make_async_copy(wk_ref, w_all.at[:, pl.ds(q_width, kv_width)], w_sem.at[1]),
        pltpu.make_async_copy(wv_ref, w_all.at[:, pl.ds(q_width + kv_width, kv_width)], w_sem.at[2]),
    )
    own_kv = (
        pltpu.make_async_copy(k_ref, kv_all.at[me, 0], w_sem.at[3]),
        pltpu.make_async_copy(v_ref, kv_all.at[me, 1], w_sem.at[4]),
    )
    row_copies = []
    for h in range(kv_local):
        for g in range(group):
            head = h * group + g
            for side, (src, dst) in enumerate(((q_ref, q_rows), (g_ref, g_rows))):
                row_copies.append(
                    pltpu.make_async_copy(
                        src.at[:, pl.ds(head * HEAD_SIZE, HEAD_SIZE)],
                        dst.at[h, pl.ds(g * tok, tok)],
                        row_sem.at[side, head],
                    )
                )
    for copy in (*own_kv, *row_copies, *weights):
        copy.start()

    barrier = pltpu.get_barrier_semaphore()

    def greet(ctx, tp):
        pl.semaphore_signal(barrier, inc=1, device_id=(ctx, tp), device_id_type=MESH)

    for dz in range(1, nz):
        greet(((z + dz) % nz) * ny + y, t)
    for dy in range(1, ny):
        greet(z * ny + (y + dy) % ny, t)
    greet(me, x * 2 + 1 - core)
    for dx in range(1, nx):
        greet(me, ((x + dx) % nx) * 2 + core)
    pl.semaphore_wait(barrier, nz - 1 + ny - 1 + 1 + nx - 1)
    for copy in own_kv:
        copy.wait()

    def up_copy(r, half):
        j = r * ny + y
        return remote(
            kv_all.at[j, half], kv_all.at[j, half], up_sem.at[r, half], kv_sem.at[j, half],
            me + ny, t,
        )

    def side_copy(r, yy, half):
        j = r * ny + y
        return remote(
            kv_all.at[j, half], kv_all.at[j, half], side_sem.at[r, yy, half], kv_sem.at[j, half],
            z * ny + yy, t,
        )

    def kv_arrival(j, half):
        remote(
            kv_all.at[j, half], kv_all.at[j, half], up_sem.at[0, half], kv_sem.at[j, half],
            me, t,
        ).wait_recv()

    power = factor * math.log2(math.e)
    head_cols = [slice(h * HEAD_SIZE, (h + 1) * HEAD_SIZE) for h in range(kv_local)]

    def forward(j, own):
        for h, cols in enumerate(head_cols):
            scores = dot(kv_all[j, 0, :, cols], q_rows[h], BY_LAST)
            if own:
                key_id = lax.broadcasted_iota(jnp.int32, (tok, rows), 0)
                query_id = lax.broadcasted_iota(jnp.int32, (tok, rows), 1) % tok
                scores = jnp.where(key_id <= query_id, scores, MASKED)
            highest = jnp.max(scores, axis=0, keepdims=True)
            raw = jnp.exp2((scores - highest) * power)
            prob_grads = dot(kv_all[j, 1, :, cols], g_rows[h], BY_LAST)
            s_scr[j, h] = raw
            p_scr[j, h] = prob_grads
            stats[j, h, 0:1] = highest
            stats[j, h, 1:2] = jnp.sum(raw, axis=0, keepdims=True)
            stats[j, h, 2:3] = jnp.sum(raw * prob_grads, axis=0, keepdims=True)

    def start_block(r, half, first):
        @pl.when((r * ny + y != deepest) & (z < nz - 1))
        def _():
            up_copy(r, half).start()

        for dy in range(1, ny):
            yy = (y + dy) % ny
            later = (y < yy) if first else True

            @pl.when((r * ny + y != deepest) & later)
            def _():
                side_copy(r, yy, half).start()

    def from_sides(r):
        for dy in range(1, ny):
            yy = (y + dy) % ny

            @pl.when(((r < z) | (yy < y)) & (r * ny + yy != deepest))
            def _():
                for half in range(2):
                    kv_arrival(r * ny + yy, half)
                forward(r * ny + yy, False)

    for half in range(2):
        start_block(z, half, True)
    depth = jnp.int32(0)
    for s in range(1, n_slots):
        depth += (anc_ref[me, s] != me).astype(jnp.int32)
    start = (depth * tok).astype(F32)
    scale = -2.0 * math.log(ROPE_BASE) / HEAD_SIZE
    which = lax.broadcasted_iota(jnp.int32, (half_head, tok), 0).astype(F32)
    place = lax.broadcasted_iota(jnp.int32, (half_head, tok), 1).astype(F32) + start
    angles = place * jnp.exp(which * scale)
    turns[0], turns[1] = jnp.cos(angles), jnp.sin(angles)
    dq_acc[...] = jnp.zeros_like(dq_acc)
    for j in range(nz * ny):
        stats[j, :, 0:1] = jnp.full((kv_local, 1, rows), MASKED, F32)
        stats[j, :, 1:3] = jnp.zeros((kv_local, 2, rows), F32)
    for copy in row_copies:
        copy.wait()
    forward(me, True)

    def gather_step(k, carry):
        r = z - k

        @pl.when(r * ny + y != deepest)
        def _():
            for half in range(2):
                kv_arrival(r * ny + y, half)
                start_block(r, half, False)
            forward(r * ny + y, False)

        from_sides(r + 1)
        return carry

    lax.fori_loop(1, z + 1, gather_step, 0)
    from_sides(jnp.int32(0))

    shifts = []
    for j in range(nz * ny):
        seen = me == j
        for s in range(1, n_slots):
            seen = seen | (anc_ref[me, s] == j)
        shifts.append(jnp.where(seen, 0.0, MASKED))
    for h in range(kv_local):
        highest = jnp.full((1, rows), MASKED, F32)
        for j in range(nz * ny):
            highest = jnp.maximum(highest, stats[j, h, 0:1] + shifts[j])
        sums = jnp.zeros((1, rows), F32)
        dots = jnp.zeros((1, rows), F32)
        for j in range(nz * ny):
            shrink = jnp.exp2((stats[j, h, 0:1] + shifts[j] - highest) * power)
            stats[j, h, 0:1] = shrink
            sums = sums + shrink * stats[j, h, 1:2]
            dots = dots + shrink * stats[j, h, 2:3]
        inverse = 1.0 / sums
        finals[h, 0:1] = inverse
        finals[h, 1:2] = dots * inverse

    def y_copy(r, yy, half):
        return remote(
            stage.at[r * ny + yy, half], yrecv.at[r, y, half],
            ys_sem.at[r, yy, half], yr_sem.at[r, y, half], z * ny + yy, t,
        )

    def y_arrival(r, yy, half):
        remote(
            stage.at[r * ny + yy, half], yrecv.at[r, yy, half],
            ys_sem.at[r, yy, half], yr_sem.at[r, yy, half], me, t,
        ).wait_recv()

    def z_copy(r, half):
        return remote(
            stage.at[r * ny + y, half], zrecv.at[z, half],
            zs_sem.at[r, half], zr_sem.at[z, half], r * ny + y, t,
        )

    def z_arrival(sz, half):
        remote(
            stage.at[me, half], zrecv.at[sz, half],
            zs_sem.at[sz, half], zr_sem.at[sz, half], me, t,
        ).wait_recv()

    def y_sends(r, yy):
        return (r <= z) & ((r < z) | (yy < y)) & (r * ny + yy != deepest)

    def backward(j):
        for h, cols in enumerate(head_cols):
            probs = s_scr[j, h] * (stats[j, h, 0:1] * finals[h, 0:1])
            score_grads = (probs * (p_scr[j, h] - finals[h, 1:2])).astype(BF16)
            stage[j, 0, :, cols] = (dot(score_grads, q_rows[h]) * factor).astype(BF16)
            stage[j, 1, :, cols] = dot(probs.astype(BF16), g_rows[h]).astype(BF16)
            dq_acc[h] += dot(kv_all[j, 0, :, cols].T, score_grads)

    def chain(r):
        j = r * ny + y
        live = j != deepest
        for half in range(2):
            total[half] = stage[j, half].astype(F32)
            for dy in range(1, ny):
                yy = (y + dy) % ny

                @pl.when(live & ((r < z) | (y < yy)))
                def _():
                    y_arrival(r, yy, half)
                    total[half] += yrecv[r, yy, half].astype(F32)

            @pl.when(live & (r < z))
            def _():
                stage[j, half] = total[half].astype(BF16)
                z_copy(r, half).start()

    def back_step(r, carry):
        for dy in range(1, ny):
            yy = (y + dy) % ny

            @pl.when(y_sends(r, yy))
            def _():
                backward(r * ny + yy)
                for half in range(2):
                    y_copy(r, yy, half).start()

        @pl.when((r * ny + y != deepest) | (r == z))
        def _():
            backward(r * ny + y)

        @pl.when((r > 0) & ((r - 1) * ny + y != deepest))
        def _():
            chain(r - 1)

        return carry

    lax.fori_loop(0, z + 1, back_step, 0)
    cos_t, sin_t = turns[0], turns[1]
    for h in range(kv_local):
        query_grad = dq_acc[h] * factor
        for g in range(group):
            one = query_grad[:, g * tok:(g + 1) * tok]
            a, b = one[:half_head], one[half_head:]
            turned = jnp.concatenate([a * cos_t + b * sin_t, b * cos_t - a * sin_t], axis=0)
            head = (h * group + g) * HEAD_SIZE
            x_all[:, head:head + HEAD_SIZE] = turned.T.astype(BF16)

    for copy in weights:
        copy.wait()
    n_chunks = acc.shape[0]

    def query_part(i, carry):
        tx = (x + 1 + i // (2 * per)) % nx
        at = tx * (2 * per) + i % (2 * per)
        w = w_all[pl.ds(pl.multiple_of(at * chunk, chunk), chunk), pl.ds(0, q_width)]
        acc[at] = dot(x_all[:, 0:q_width], w, BY_LAST)
        return carry

    early = jnp.where(z == nz - 1, n_chunks - 2 * per, n_chunks)
    lax.fori_loop(0, early, query_part, 0)
    chain(z)

    def from_above(sz, carry):
        for half in range(2):
            z_arrival(sz, half)
            total[half] += zrecv[sz, half].astype(F32)
        return carry

    lax.fori_loop(z + 1, jnp.where(me == deepest, z + 1, nz), from_above, 0)

    both_cos = jnp.concatenate([cos_t, cos_t], axis=0).T
    both_sin = jnp.concatenate([sin_t, -sin_t], axis=0).T
    for h in range(kv_local):
        one = total[0, :, h * HEAD_SIZE:(h + 1) * HEAD_SIZE]
        swapped = jnp.concatenate([one[:, half_head:], one[:, :half_head]], axis=1)
        at = q_width + h * HEAD_SIZE
        x_all[:, at:at + HEAD_SIZE] = (one * both_cos + swapped * both_sin).astype(BF16)
    x_all[:, q_width + kv_width:] = total[1].astype(BF16)

    def piece(target, i):
        at = target * per + i
        w = w_all[pl.ds(pl.multiple_of(at * chunk, chunk), chunk), pl.ds(q_width, 2 * kv_width)]
        return acc[at] + dot(x_all[:, q_width:], w, BY_LAST)

    def sib_copy(tx, i):
        return remote(
            sib_send.at[tx, i], sib_recv.at[tx, i], ss_sem.at[tx, i], sr_sem.at[tx, i],
            me, x * 2 + 1 - core,
        )

    def x_copy(tx, i):
        return remote(
            x_send.at[tx, i], x_recv.at[x, i], xs_sem.at[tx, i], xr_sem.at[x, i],
            me, tx * 2 + core,
        )

    def x_arrival(sx, i):
        remote(
            x_send.at[sx, i], x_recv.at[sx, i], xs_sem.at[sx, i], xr_sem.at[sx, i], me, t
        ).wait_recv()

    def to_sibling(tx):
        def body(i, carry):
            sib_send[tx, i] = piece(tx * 2 + 1 - core, i).astype(BF16)
            sib_copy(tx, i).start()
            return carry

        lax.fori_loop(0, per, body, 0)

    def from_sibling(tx, i):
        part = piece(tx * 2 + core, i)
        sib_copy(tx, i).wait_recv()
        return part + sib_recv[tx, i].astype(F32)

    for dx in range(1, nx):
        tx = (x + dx) % nx
        to_sibling(tx)

        def across(i, carry):
            x_send[tx, i] = from_sibling(tx, i).astype(BF16)
            x_copy(tx, i).start()
            return carry

        lax.fori_loop(0, per, across, 0)
    lax.fori_loop(early, n_chunks, query_part, 0)
    to_sibling(x)

    def last(i, carry):
        result = from_sibling(x, i)
        for dx in range(1, nx):
            sx = (x + dx) % nx
            x_arrival(sx, i)
            result = result + x_recv[sx, i].astype(F32)
        out_ref[:, pl.ds(pl.multiple_of(i * chunk, chunk), chunk)] = result.astype(BF16)
        return carry

    lax.fori_loop(0, per, last, 0)

    for k in range(nz):
        r = z - k
        live = (r >= 0) & (r * ny + y != deepest)
        for half in range(2):
            @pl.when(live & (z < nz - 1))
            def _():
                up_copy(r, half).wait_send()

            for dy in range(1, ny):
                yy = (y + dy) % ny

                @pl.when(live & ((k > 0) | (y < yy)))
                def _():
                    side_copy(r, yy, half).wait_send()
    for r in range(nz):
        for half in range(2):
            for dy in range(1, ny):
                yy = (y + dy) % ny

                @pl.when(y_sends(r, yy))
                def _():
                    y_copy(r, yy, half).wait_send()

            @pl.when((r < z) & (r * ny + y != deepest))
            def _():
                z_copy(r, half).wait_send()

    def drain(i, carry):
        for tx in range(nx):
            sib_copy(tx, i).wait_send()
        for dx in range(1, nx):
            x_copy((x + dx) % nx, i).wait_send()
        return carry

    lax.fori_loop(0, per, drain, 0)


def shards(nz, ny, nx, queries, keys, values, out_grad, ancestry, w_query, key_matrix, value_matrix):
    n = nz * ny
    tok, q_width = queries.shape
    kv_width = keys.shape[1]
    kv_local = kv_width // HEAD_SIZE
    rows = tok * (q_width // kv_width)
    model = w_query.shape[0]
    wide = model // (2 * nx)
    chunk = 256 if wide % 256 == 0 else 128
    per = wide // chunk
    pair = (2, tok, kv_width)
    dma = pltpu.SemaphoreType.DMA
    vmem = pl.BlockSpec(memory_space=pltpu.VMEM)
    hbm = pl.BlockSpec(memory_space=pl.ANY)
    return pl.pallas_call(
        functools.partial(kernel, nz, ny, nx),
        out_shape=jax.ShapeDtypeStruct((tok, wide), BF16),
        in_specs=[pl.BlockSpec(memory_space=pltpu.SMEM)] + [hbm] * 7,
        out_specs=vmem,
        scratch_shapes=[
            pltpu.VMEM((model, q_width + 2 * kv_width), BF16),
            pltpu.VMEM((n,) + pair, BF16),
            pltpu.VMEM((kv_local, rows, HEAD_SIZE), BF16),
            pltpu.VMEM((kv_local, rows, HEAD_SIZE), BF16),
            pltpu.VMEM((n, kv_local, tok, rows), F32),
            pltpu.VMEM((n, kv_local, tok, rows), F32),
            pltpu.VMEM((n, kv_local, 8, rows), F32),
            pltpu.VMEM((kv_local, 8, rows), F32),
            pltpu.VMEM((2, HEAD_SIZE // 2, tok), F32),
            pltpu.VMEM((kv_local, HEAD_SIZE, rows), F32),
            pltpu.VMEM((n,) + pair, BF16),
            pltpu.VMEM((nz, ny) + pair, BF16),
            pltpu.VMEM((nz,) + pair, BF16),
            pltpu.VMEM(pair, F32),
            pltpu.VMEM((tok, q_width + 2 * kv_width), BF16),
            pltpu.VMEM((model // chunk, tok, chunk), F32),
            pltpu.VMEM((nx, per, tok, chunk), BF16),
            pltpu.VMEM((nx, per, tok, chunk), BF16),
            pltpu.VMEM((nx, per, tok, chunk), BF16),
            pltpu.VMEM((nx, per, tok, chunk), BF16),
            dma((5,)), dma((2, q_width // HEAD_SIZE)), dma((nz, 2)), dma((nz, ny, 2)), dma((n, 2)),
            dma((nz, ny, 2)), dma((nz, ny, 2)), dma((nz, 2)), dma((nz, 2)),
            dma((nx, per)), dma((nx, per)), dma((nx, per)), dma((nx, per)),
        ],
        compiler_params=pltpu.CompilerParams(
            collective_id=0, has_side_effects=True, vmem_limit_bytes=60 * 1024 * 1024
        ),
        name="tree_attention_backward",
    )(ancestry, queries, keys, values, out_grad, w_query, key_matrix, value_matrix)


def solution(mesh):
    n = mesh.shape["ctx"]
    ny = 2 ** ((n.bit_length() - 1) // 2)
    nx = mesh.shape["tp"] // 2
    in_specs = (
        P("ctx", "tp"),
        P("ctx", "tp"),
        P("ctx", "tp"),
        P("ctx", "tp"),
        P(),
        P(None, "tp"),
        P(None, "tp"),
        P(None, "tp"),
    )
    return jax.shard_map(
        functools.partial(shards, n // ny, ny, nx),
        mesh=mesh, in_specs=in_specs, out_specs=P("ctx", "tp"), check_vma=False,
    )
```

```python
import functools
import math

import jax
import jax.numpy as jnp
from jax import lax
from jax.experimental import pallas as pl
from jax.experimental.pallas import tpu as pltpu
from jax.sharding import PartitionSpec as P

HEAD_SIZE = 128
ROPE_BASE = 1000000.0
MASKED = -1e30
MESH = pl.DeviceIdType.MESH
F32 = jnp.float32
BF16 = jnp.bfloat16
BY_LAST = (((1,), (1,)), ((), ()))
PLAIN = (((1,), (0,)), ((), ()))


def dot(a, b, contract=PLAIN):
    return lax.dot_general(a, b, contract, preferred_element_type=F32)


def kernel(
    nz, ny, nx,
    anc_ref, q_ref, k_ref, v_ref, g_ref, wq_ref, wk_ref, wv_ref, out_ref,
    w_all, kv_all, q_rows, g_rows, s_scr, p_scr, stats, finals, turns, dq_acc, stage, yrecv, zrecv, total,
    x_t, acc, sib_send, sib_recv, x_send, x_recv,
    w_sem, row_sem, up_sem, side_sem, kv_sem, ys_sem, yr_sem, zs_sem, zr_sem,
    ss_sem, sr_sem, xs_sem, xr_sem,
):
    tok, q_width = q_ref.shape
    kv_width = k_ref.shape[1]
    kv_local = kv_width // HEAD_SIZE
    group = q_width // kv_width
    rows = group * tok
    n_slots = anc_ref.shape[1]
    deepest = n_slots - 1
    factor = HEAD_SIZE ** -0.5
    half_head = HEAD_SIZE // 2
    chunk = sib_send.shape[2]
    wide = out_ref.shape[1]
    per = wide // chunk

    me, t = lax.axis_index("ctx"), lax.axis_index("tp")
    z, y = me // ny, me % ny
    x, core = t // 2, t % 2

    def remote(src, dst, send, recv, ctx, tp):
        return pltpu.make_async_remote_copy(
            src_ref=src, dst_ref=dst, send_sem=send, recv_sem=recv,
            device_id=(ctx, tp), device_id_type=MESH,
        )

    weights = (
        pltpu.make_async_copy(wq_ref, w_all.at[:, pl.ds(0, q_width)], w_sem.at[0]),
        pltpu.make_async_copy(wk_ref, w_all.at[:, pl.ds(q_width, kv_width)], w_sem.at[1]),
        pltpu.make_async_copy(wv_ref, w_all.at[:, pl.ds(q_width + kv_width, kv_width)], w_sem.at[2]),
    )
    own_kv = (
        pltpu.make_async_copy(k_ref, kv_all.at[me, 0], w_sem.at[3]),
        pltpu.make_async_copy(v_ref, kv_all.at[me, 1], w_sem.at[4]),
    )
    row_copies = []
    for h in range(kv_local):
        for g in range(group):
            head = h * group + g
            for side, (src, dst) in enumerate(((q_ref, q_rows), (g_ref, g_rows))):
                row_copies.append(
                    pltpu.make_async_copy(
                        src.at[:, pl.ds(head * HEAD_SIZE, HEAD_SIZE)],
                        dst.at[h, pl.ds(g * tok, tok)],
                        row_sem.at[side, head],
                    )
                )
    for copy in (*own_kv, *row_copies, *weights):
        copy.start()

    barrier = pltpu.get_barrier_semaphore()

    def greet(ctx, tp):
        pl.semaphore_signal(barrier, inc=1, device_id=(ctx, tp), device_id_type=MESH)

    for dz in range(1, nz):
        greet(((z + dz) % nz) * ny + y, t)
    for dy in range(1, ny):
        greet(z * ny + (y + dy) % ny, t)
    greet(me, x * 2 + 1 - core)
    for dx in range(1, nx):
        greet(me, ((x + dx) % nx) * 2 + core)
    pl.semaphore_wait(barrier, nz - 1 + ny - 1 + 1 + nx - 1)
    for copy in own_kv:
        copy.wait()

    def up_copy(r, half):
        j = r * ny + y
        return remote(
            kv_all.at[j, half], kv_all.at[j, half], up_sem.at[r, half], kv_sem.at[j, half],
            me + ny, t,
        )

    def side_copy(r, yy, half):
        j = r * ny + y
        return remote(
            kv_all.at[j, half], kv_all.at[j, half], side_sem.at[r, yy, half], kv_sem.at[j, half],
            z * ny + yy, t,
        )

    def kv_arrival(j, half):
        remote(
            kv_all.at[j, half], kv_all.at[j, half], up_sem.at[0, half], kv_sem.at[j, half],
            me, t,
        ).wait_recv()

    power = factor * math.log2(math.e)
    head_cols = [slice(h * HEAD_SIZE, (h + 1) * HEAD_SIZE) for h in range(kv_local)]

    def forward(j, own):
        for h, cols in enumerate(head_cols):
            scores = dot(kv_all[j, 0, :, cols], q_rows[h], BY_LAST)
            if own:
                key_id = lax.broadcasted_iota(jnp.int32, (tok, rows), 0)
                query_id = lax.broadcasted_iota(jnp.int32, (tok, rows), 1) % tok
                scores = jnp.where(key_id <= query_id, scores, MASKED)
            highest = jnp.max(scores, axis=0, keepdims=True)
            raw = jnp.exp2((scores - highest) * power)
            prob_grads = dot(kv_all[j, 1, :, cols], g_rows[h], BY_LAST)
            s_scr[j, h] = raw
            p_scr[j, h] = prob_grads
            stats[j, h, 0:1] = highest
            stats[j, h, 1:2] = jnp.sum(raw, axis=0, keepdims=True)
            stats[j, h, 2:3] = jnp.sum(raw * prob_grads, axis=0, keepdims=True)

    def start_block(r, half, first):
        @pl.when((r * ny + y != deepest) & (z < nz - 1))
        def _():
            up_copy(r, half).start()

        for dy in range(1, ny):
            yy = (y + dy) % ny
            later = (y < yy) if first else True

            @pl.when((r * ny + y != deepest) & later)
            def _():
                side_copy(r, yy, half).start()

    def from_sides(r):
        for dy in range(1, ny):
            yy = (y + dy) % ny

            @pl.when(((r < z) | (yy < y)) & (r * ny + yy != deepest))
            def _():
                for half in range(2):
                    kv_arrival(r * ny + yy, half)
                forward(r * ny + yy, False)

    for half in range(2):
        start_block(z, half, True)
    depth = jnp.int32(0)
    for s in range(1, n_slots):
        depth += (anc_ref[me, s] != me).astype(jnp.int32)
    start = (depth * tok).astype(F32)
    scale = -2.0 * math.log(ROPE_BASE) / HEAD_SIZE
    which = lax.broadcasted_iota(jnp.int32, (half_head, tok), 0).astype(F32)
    place = lax.broadcasted_iota(jnp.int32, (half_head, tok), 1).astype(F32) + start
    angles = place * jnp.exp(which * scale)
    turns[0], turns[1] = jnp.cos(angles), jnp.sin(angles)
    dq_acc[...] = jnp.zeros_like(dq_acc)
    for j in range(nz * ny):
        stats[j, :, 0:1] = jnp.full((kv_local, 1, rows), MASKED, F32)
        stats[j, :, 1:3] = jnp.zeros((kv_local, 2, rows), F32)
    for copy in row_copies:
        copy.wait()
    forward(me, True)

    def gather_step(k, carry):
        r = z - k

        @pl.when(r * ny + y != deepest)
        def _():
            for half in range(2):
                kv_arrival(r * ny + y, half)
                start_block(r, half, False)
            forward(r * ny + y, False)

        from_sides(r + 1)
        return carry

    lax.fori_loop(1, z + 1, gather_step, 0)
    from_sides(jnp.int32(0))

    shifts = []
    for j in range(nz * ny):
        seen = me == j
        for s in range(1, n_slots):
            seen = seen | (anc_ref[me, s] == j)
        shifts.append(jnp.where(seen, 0.0, MASKED))
    for h in range(kv_local):
        highest = jnp.full((1, rows), MASKED, F32)
        for j in range(nz * ny):
            highest = jnp.maximum(highest, stats[j, h, 0:1] + shifts[j])
        sums = jnp.zeros((1, rows), F32)
        dots = jnp.zeros((1, rows), F32)
        for j in range(nz * ny):
            shrink = jnp.exp2((stats[j, h, 0:1] + shifts[j] - highest) * power)
            stats[j, h, 0:1] = shrink
            sums = sums + shrink * stats[j, h, 1:2]
            dots = dots + shrink * stats[j, h, 2:3]
        inverse = 1.0 / sums
        finals[h, 0:1] = inverse
        finals[h, 1:2] = dots * inverse

    def y_copy(r, yy, half):
        return remote(
            stage.at[r * ny + yy, half], yrecv.at[r, y, half],
            ys_sem.at[r, yy, half], yr_sem.at[r, y, half], z * ny + yy, t,
        )

    def y_arrival(r, yy, half):
        remote(
            stage.at[r * ny + yy, half], yrecv.at[r, yy, half],
            ys_sem.at[r, yy, half], yr_sem.at[r, yy, half], me, t,
        ).wait_recv()

    def z_copy(r, half):
        return remote(
            stage.at[r * ny + y, half], zrecv.at[z, half],
            zs_sem.at[r, half], zr_sem.at[z, half], r * ny + y, t,
        )

    def z_arrival(sz, half):
        remote(
            stage.at[me, half], zrecv.at[sz, half],
            zs_sem.at[sz, half], zr_sem.at[sz, half], me, t,
        ).wait_recv()

    def y_sends(r, yy):
        return (r <= z) & ((r < z) | (yy < y)) & (r * ny + yy != deepest)

    def backward(j):
        for h, cols in enumerate(head_cols):
            probs = s_scr[j, h] * (stats[j, h, 0:1] * finals[h, 0:1])
            score_grads = (probs * (p_scr[j, h] - finals[h, 1:2])).astype(BF16)
            stage[j, 0, :, cols] = (dot(score_grads, q_rows[h]) * factor).astype(BF16)
            stage[j, 1, :, cols] = dot(probs.astype(BF16), g_rows[h]).astype(BF16)
            dq_acc[h] += dot(kv_all[j, 0, :, cols].T, score_grads)

    def chain(r):
        j = r * ny + y
        live = j != deepest
        for half in range(2):
            total[half] = stage[j, half].astype(F32)
            for dy in range(1, ny):
                yy = (y + dy) % ny

                @pl.when(live & ((r < z) | (y < yy)))
                def _():
                    y_arrival(r, yy, half)
                    total[half] += yrecv[r, yy, half].astype(F32)

            @pl.when(live & (r < z))
            def _():
                stage[j, half] = total[half].astype(BF16)
                z_copy(r, half).start()

    def back_step(r, carry):
        for dy in range(1, ny):
            yy = (y + dy) % ny

            @pl.when(y_sends(r, yy))
            def _():
                backward(r * ny + yy)
                for half in range(2):
                    y_copy(r, yy, half).start()

        @pl.when((r * ny + y != deepest) | (r == z))
        def _():
            backward(r * ny + y)

        @pl.when((r > 0) & ((r - 1) * ny + y != deepest))
        def _():
            chain(r - 1)

        return carry

    lax.fori_loop(0, z + 1, back_step, 0)
    cos_t, sin_t = turns[0], turns[1]
    for h in range(kv_local):
        query_grad = dq_acc[h] * factor
        for g in range(group):
            one = query_grad[:, g * tok:(g + 1) * tok]
            a, b = one[:half_head], one[half_head:]
            turned = jnp.concatenate([a * cos_t + b * sin_t, b * cos_t - a * sin_t], axis=0)
            head = (h * group + g) * HEAD_SIZE
            x_t[head:head + HEAD_SIZE, :] = turned.astype(BF16)

    for copy in weights:
        copy.wait()
    def quarter_at(target):
        return pl.ds(pl.multiple_of(target * wide, HEAD_SIZE), wide)

    def query_part(i, carry):
        at = quarter_at(((x + 1 + i // 2) % nx) * 2 + i % 2)
        acc[at] = dot(w_all[at, 0:q_width], x_t[0:q_width])
        return carry

    early = jnp.where(z == nz - 1, 2 * nx - 2, 2 * nx)
    lax.fori_loop(0, early, query_part, 0)
    chain(z)

    def from_above(sz, carry):
        for half in range(2):
            z_arrival(sz, half)
            total[half] += zrecv[sz, half].astype(F32)
        return carry

    lax.fori_loop(z + 1, jnp.where(me == deepest, z + 1, nz), from_above, 0)

    for h, cols in enumerate(head_cols):
        one = total[0, :, cols].T
        a, b = one[:half_head], one[half_head:]
        turned = jnp.concatenate([a * cos_t + b * sin_t, b * cos_t - a * sin_t], axis=0)
        at = q_width + h * HEAD_SIZE
        x_t[at:at + HEAD_SIZE, :] = turned.astype(BF16)
        at = at + kv_width
        x_t[at:at + HEAD_SIZE, :] = total[1, :, cols].T.astype(BF16)

    def key_value_part(target):
        at = quarter_at(target)
        acc[at] += dot(w_all[at, q_width:], x_t[q_width:])

    def piece(target, i):
        return acc[pl.ds(pl.multiple_of(target * wide + i * chunk, HEAD_SIZE), chunk)]

    def sib_copy(tx, i):
        return remote(
            sib_send.at[tx, i], sib_recv.at[tx, i], ss_sem.at[tx, i], sr_sem.at[tx, i],
            me, x * 2 + 1 - core,
        )

    def x_copy(tx, i):
        return remote(
            x_send.at[tx, i], x_recv.at[x, i], xs_sem.at[tx, i], xr_sem.at[x, i],
            me, tx * 2 + core,
        )

    def x_arrival(sx, i):
        remote(
            x_send.at[sx, i], x_recv.at[sx, i], xs_sem.at[sx, i], xr_sem.at[sx, i], me, t
        ).wait_recv()

    def to_sibling(tx):
        key_value_part(tx * 2 + 1 - core)

        def body(i, carry):
            sib_send[tx, i] = piece(tx * 2 + 1 - core, i).astype(BF16)
            sib_copy(tx, i).start()
            return carry

        lax.fori_loop(0, per, body, 0)

    def from_sibling(tx, i):
        part = piece(tx * 2 + core, i)
        sib_copy(tx, i).wait_recv()
        return part + sib_recv[tx, i].astype(F32)

    for dx in range(1, nx):
        tx = (x + dx) % nx
        to_sibling(tx)
        key_value_part(tx * 2 + core)

        def across(i, carry):
            x_send[tx, i] = from_sibling(tx, i).astype(BF16)
            x_copy(tx, i).start()
            return carry

        lax.fori_loop(0, per, across, 0)
    lax.fori_loop(early, 2 * nx, query_part, 0)
    to_sibling(x)
    key_value_part(x * 2 + core)

    def last(i, carry):
        result = from_sibling(x, i)
        for dx in range(1, nx):
            sx = (x + dx) % nx
            x_arrival(sx, i)
            result = result + x_recv[sx, i].astype(F32)
        out_ref[:, pl.ds(pl.multiple_of(i * chunk, chunk), chunk)] = result.T.astype(BF16)
        return carry

    lax.fori_loop(0, per, last, 0)

    for k in range(nz):
        r = z - k
        live = (r >= 0) & (r * ny + y != deepest)
        for half in range(2):
            @pl.when(live & (z < nz - 1))
            def _():
                up_copy(r, half).wait_send()

            for dy in range(1, ny):
                yy = (y + dy) % ny

                @pl.when(live & ((k > 0) | (y < yy)))
                def _():
                    side_copy(r, yy, half).wait_send()
    for r in range(nz):
        for half in range(2):
            for dy in range(1, ny):
                yy = (y + dy) % ny

                @pl.when(y_sends(r, yy))
                def _():
                    y_copy(r, yy, half).wait_send()

            @pl.when((r < z) & (r * ny + y != deepest))
            def _():
                z_copy(r, half).wait_send()

    def drain(i, carry):
        for tx in range(nx):
            sib_copy(tx, i).wait_send()
        for dx in range(1, nx):
            x_copy((x + dx) % nx, i).wait_send()
        return carry

    lax.fori_loop(0, per, drain, 0)


def shards(nz, ny, nx, queries, keys, values, out_grad, ancestry, w_query, key_matrix, value_matrix):
    n = nz * ny
    tok, q_width = queries.shape
    kv_width = keys.shape[1]
    kv_local = kv_width // HEAD_SIZE
    rows = tok * (q_width // kv_width)
    model = w_query.shape[0]
    wide = model // (2 * nx)
    chunk = 256 if wide % 256 == 0 else 128
    per = wide // chunk
    pair = (2, tok, kv_width)
    dma = pltpu.SemaphoreType.DMA
    vmem = pl.BlockSpec(memory_space=pltpu.VMEM)
    hbm = pl.BlockSpec(memory_space=pl.ANY)
    return pl.pallas_call(
        functools.partial(kernel, nz, ny, nx),
        out_shape=jax.ShapeDtypeStruct((tok, wide), BF16),
        in_specs=[pl.BlockSpec(memory_space=pltpu.SMEM)] + [hbm] * 7,
        out_specs=vmem,
        scratch_shapes=[
            pltpu.VMEM((model, q_width + 2 * kv_width), BF16),
            pltpu.VMEM((n,) + pair, BF16),
            pltpu.VMEM((kv_local, rows, HEAD_SIZE), BF16),
            pltpu.VMEM((kv_local, rows, HEAD_SIZE), BF16),
            pltpu.VMEM((n, kv_local, tok, rows), F32),
            pltpu.VMEM((n, kv_local, tok, rows), F32),
            pltpu.VMEM((n, kv_local, 8, rows), F32),
            pltpu.VMEM((kv_local, 8, rows), F32),
            pltpu.VMEM((2, HEAD_SIZE // 2, tok), F32),
            pltpu.VMEM((kv_local, HEAD_SIZE, rows), F32),
            pltpu.VMEM((n,) + pair, BF16),
            pltpu.VMEM((nz, ny) + pair, BF16),
            pltpu.VMEM((nz,) + pair, BF16),
            pltpu.VMEM(pair, F32),
            pltpu.VMEM((q_width + 2 * kv_width, tok), BF16),
            pltpu.VMEM((model, tok), F32),
            pltpu.VMEM((nx, per, chunk, tok), BF16),
            pltpu.VMEM((nx, per, chunk, tok), BF16),
            pltpu.VMEM((nx, per, chunk, tok), BF16),
            pltpu.VMEM((nx, per, chunk, tok), BF16),
            dma((5,)), dma((2, q_width // HEAD_SIZE)), dma((nz, 2)), dma((nz, ny, 2)), dma((n, 2)),
            dma((nz, ny, 2)), dma((nz, ny, 2)), dma((nz, 2)), dma((nz, 2)),
            dma((nx, per)), dma((nx, per)), dma((nx, per)), dma((nx, per)),
        ],
        compiler_params=pltpu.CompilerParams(
            collective_id=0, has_side_effects=True, vmem_limit_bytes=60 * 1024 * 1024
        ),
        name="tree_attention_backward",
    )(ancestry, queries, keys, values, out_grad, w_query, key_matrix, value_matrix)


def solution(mesh):
    n = mesh.shape["ctx"]
    ny = 2 ** ((n.bit_length() - 1) // 2)
    nx = mesh.shape["tp"] // 2
    in_specs = (
        P("ctx", "tp"),
        P("ctx", "tp"),
        P("ctx", "tp"),
        P("ctx", "tp"),
        P(),
        P(None, "tp"),
        P(None, "tp"),
        P(None, "tp"),
    )
    return jax.shard_map(
        functools.partial(shards, n // ny, ny, nx),
        mesh=mesh, in_specs=in_specs, out_specs=P("ctx", "tp"), check_vma=False,
    )
```

```python
import functools
import math

import jax
import jax.numpy as jnp
from jax import lax
from jax.experimental import pallas as pl
from jax.experimental.pallas import tpu as pltpu
from jax.sharding import PartitionSpec as P

HEAD_SIZE = 128
ROPE_BASE = 1000000.0
MASKED = -1e30
MESH = pl.DeviceIdType.MESH
F32 = jnp.float32
BF16 = jnp.bfloat16
BY_LAST = (((1,), (1,)), ((), ()))
PLAIN = (((1,), (0,)), ((), ()))


def dot(a, b, contract=PLAIN):
    return lax.dot_general(a, b, contract, preferred_element_type=F32)


def kernel(
    nz, ny, nx,
    anc_ref, q_ref, k_ref, v_ref, g_ref, wq_ref, wk_ref, wv_ref, out_ref,
    w_all, kv_all, q_rows, g_rows, s_scr, p_scr, stats, finals, turns, dq_acc, stage, yrecv, zrecv, total,
    x_t, acc, sib_send, sib_recv, x_send, x_recv,
    w_sem, row_sem, up_sem, side_sem, kv_sem, ys_sem, yr_sem, zs_sem, zr_sem,
    ss_sem, sr_sem, xs_sem, xr_sem,
):
    tok, q_width = q_ref.shape
    kv_width = k_ref.shape[1]
    kv_local = kv_width // HEAD_SIZE
    group = q_width // kv_width
    rows = group * tok
    n_slots = anc_ref.shape[1]
    deepest = n_slots - 1
    factor = HEAD_SIZE ** -0.5
    half_head = HEAD_SIZE // 2
    chunk = sib_send.shape[2]
    wide = out_ref.shape[1]
    per = wide // chunk

    me, t = lax.axis_index("ctx"), lax.axis_index("tp")
    z, y = me // ny, me % ny
    x, core = t // 2, t % 2

    def remote(src, dst, send, recv, ctx, tp):
        return pltpu.make_async_remote_copy(
            src_ref=src, dst_ref=dst, send_sem=send, recv_sem=recv,
            device_id=(ctx, tp), device_id_type=MESH,
        )

    weights = (
        pltpu.make_async_copy(wq_ref, w_all.at[:, pl.ds(0, q_width)], w_sem.at[0]),
        pltpu.make_async_copy(wk_ref, w_all.at[:, pl.ds(q_width, kv_width)], w_sem.at[1]),
        pltpu.make_async_copy(wv_ref, w_all.at[:, pl.ds(q_width + kv_width, kv_width)], w_sem.at[2]),
    )
    own_kv = (
        pltpu.make_async_copy(k_ref, kv_all.at[me, 0], w_sem.at[3]),
        pltpu.make_async_copy(v_ref, kv_all.at[me, 1], w_sem.at[4]),
    )
    row_copies = []
    for h in range(kv_local):
        for g in range(group):
            head = h * group + g
            for side, (src, dst) in enumerate(((q_ref, q_rows), (g_ref, g_rows))):
                row_copies.append(
                    pltpu.make_async_copy(
                        src.at[:, pl.ds(head * HEAD_SIZE, HEAD_SIZE)],
                        dst.at[h, pl.ds(g * tok, tok)],
                        row_sem.at[side, head],
                    )
                )
    for copy in (*own_kv, *row_copies, *weights):
        copy.start()

    barrier = pltpu.get_barrier_semaphore()

    def greet(ctx, tp):
        pl.semaphore_signal(barrier, inc=1, device_id=(ctx, tp), device_id_type=MESH)

    for dz in range(1, nz):
        greet(((z + dz) % nz) * ny + y, t)
    for dy in range(1, ny):
        greet(z * ny + (y + dy) % ny, t)
    greet(me, x * 2 + 1 - core)
    for dx in range(1, nx):
        greet(me, ((x + dx) % nx) * 2 + core)
    if deepest < nz * ny:
        @pl.when(me != deepest)
        def _():
            kv_all[deepest] = jnp.zeros_like(kv_all[deepest])

    pl.semaphore_wait(barrier, nz - 1 + ny - 1 + 1 + nx - 1)
    for copy in own_kv:
        copy.wait()

    def up_copy(r, half):
        j = r * ny + y
        return remote(
            kv_all.at[j, half], kv_all.at[j, half], up_sem.at[r, half], kv_sem.at[j, half],
            me + ny, t,
        )

    def side_copy(r, yy, half):
        j = r * ny + y
        return remote(
            kv_all.at[j, half], kv_all.at[j, half], side_sem.at[r, yy, half], kv_sem.at[j, half],
            z * ny + yy, t,
        )

    def kv_arrival(j, half):
        remote(
            kv_all.at[j, half], kv_all.at[j, half], up_sem.at[0, half], kv_sem.at[j, half],
            me, t,
        ).wait_recv()

    power = factor * math.log2(math.e)
    head_cols = [slice(h * HEAD_SIZE, (h + 1) * HEAD_SIZE) for h in range(kv_local)]

    def forward(j, own):
        for h, cols in enumerate(head_cols):
            scores = dot(kv_all[j, 0, :, cols], q_rows[h], BY_LAST)
            if own:
                key_id = lax.broadcasted_iota(jnp.int32, (tok, rows), 0)
                query_id = lax.broadcasted_iota(jnp.int32, (tok, rows), 1) % tok
                scores = jnp.where(key_id <= query_id, scores, MASKED)
            highest = jnp.max(scores, axis=0, keepdims=True)
            raw = jnp.exp2((scores - highest) * power)
            prob_grads = dot(kv_all[j, 1, :, cols], g_rows[h], BY_LAST)
            s_scr[j, h] = raw
            p_scr[j, h] = prob_grads
            stats[j, h, 0:1] = highest
            stats[j, h, 1:2] = jnp.sum(raw, axis=0, keepdims=True)
            stats[j, h, 2:3] = jnp.sum(raw * prob_grads, axis=0, keepdims=True)

    def forward_row(r):
        pack = pl.ds(r * ny, ny)
        for h, cols in enumerate(head_cols):
            keys = kv_all[pack, 0, :, cols].reshape(ny * tok, HEAD_SIZE)
            values = kv_all[pack, 1, :, cols].reshape(ny * tok, HEAD_SIZE)
            scores = dot(keys, q_rows[h], BY_LAST).reshape(ny, tok, rows)
            highest = jnp.max(scores, axis=1, keepdims=True)
            raw = jnp.exp2((scores - highest) * power)
            prob_grads = dot(values, g_rows[h], BY_LAST).reshape(ny, tok, rows)
            s_scr[pack, h] = raw
            p_scr[pack, h] = prob_grads
            stats[pack, h, 0:1] = highest
            stats[pack, h, 1:2] = jnp.sum(raw, axis=1, keepdims=True)
            stats[pack, h, 2:3] = jnp.sum(raw * prob_grads, axis=1, keepdims=True)

    def start_block(r, half, first):
        @pl.when((r * ny + y != deepest) & (z < nz - 1))
        def _():
            up_copy(r, half).start()

        for dy in range(1, ny):
            yy = (y + dy) % ny
            later = (y < yy) if first else True

            @pl.when((r * ny + y != deepest) & later)
            def _():
                side_copy(r, yy, half).start()

    def from_sides(r):
        for dy in range(1, ny):
            yy = (y + dy) % ny

            @pl.when(((r < z) | (yy < y)) & (r * ny + yy != deepest))
            def _():
                for half in range(2):
                    kv_arrival(r * ny + yy, half)

                @pl.when(r == z)
                def _():
                    forward(r * ny + yy, False)

        @pl.when(r < z)
        def _():
            forward_row(r)

    for half in range(2):
        start_block(z, half, True)
    depth = jnp.int32(0)
    for s in range(1, n_slots):
        depth += (anc_ref[me, s] != me).astype(jnp.int32)
    start = (depth * tok).astype(F32)
    scale = -2.0 * math.log(ROPE_BASE) / HEAD_SIZE
    which = lax.broadcasted_iota(jnp.int32, (half_head, tok), 0).astype(F32)
    place = lax.broadcasted_iota(jnp.int32, (half_head, tok), 1).astype(F32) + start
    angles = place * jnp.exp(which * scale)
    turns[0], turns[1] = jnp.cos(angles), jnp.sin(angles)
    dq_acc[...] = jnp.zeros_like(dq_acc)
    for j in range(nz * ny):
        stats[j, :, 0:1] = jnp.full((kv_local, 1, rows), MASKED, F32)
        stats[j, :, 1:3] = jnp.zeros((kv_local, 2, rows), F32)
    for copy in row_copies:
        copy.wait()
    forward(me, True)

    def gather_step(k, carry):
        r = z - k

        @pl.when(r * ny + y != deepest)
        def _():
            for half in range(2):
                kv_arrival(r * ny + y, half)
                start_block(r, half, False)

        from_sides(r + 1)
        return carry

    lax.fori_loop(1, z + 1, gather_step, 0)
    from_sides(jnp.int32(0))

    shifts = []
    for j in range(nz * ny):
        seen = me == j
        for s in range(1, n_slots):
            seen = seen | (anc_ref[me, s] == j)
        shifts.append(jnp.where(seen, 0.0, MASKED))
    for h in range(kv_local):
        highest = jnp.full((1, rows), MASKED, F32)
        for j in range(nz * ny):
            highest = jnp.maximum(highest, stats[j, h, 0:1] + shifts[j])
        sums = jnp.zeros((1, rows), F32)
        dots = jnp.zeros((1, rows), F32)
        for j in range(nz * ny):
            shrink = jnp.exp2((stats[j, h, 0:1] + shifts[j] - highest) * power)
            stats[j, h, 0:1] = shrink
            sums = sums + shrink * stats[j, h, 1:2]
            dots = dots + shrink * stats[j, h, 2:3]
        inverse = 1.0 / sums
        finals[h, 0:1] = inverse
        finals[h, 1:2] = dots * inverse

    def y_copy(r, yy, half):
        return remote(
            stage.at[r * ny + yy, half], yrecv.at[r, y, half],
            ys_sem.at[r, yy, half], yr_sem.at[r, y, half], z * ny + yy, t,
        )

    def y_arrival(r, yy, half):
        remote(
            stage.at[r * ny + yy, half], yrecv.at[r, yy, half],
            ys_sem.at[r, yy, half], yr_sem.at[r, yy, half], me, t,
        ).wait_recv()

    def z_copy(r, half):
        return remote(
            stage.at[r * ny + y, half], zrecv.at[z, half],
            zs_sem.at[r, half], zr_sem.at[z, half], r * ny + y, t,
        )

    def z_arrival(sz, half):
        remote(
            stage.at[me, half], zrecv.at[sz, half],
            zs_sem.at[sz, half], zr_sem.at[sz, half], me, t,
        ).wait_recv()

    def y_sends(r, yy):
        return (r <= z) & ((r < z) | (yy < y)) & (r * ny + yy != deepest)

    def backward(j):
        for h, cols in enumerate(head_cols):
            probs = s_scr[j, h] * (stats[j, h, 0:1] * finals[h, 0:1])
            score_grads = (probs * (p_scr[j, h] - finals[h, 1:2])).astype(BF16)
            stage[j, 0, :, cols] = (dot(score_grads, q_rows[h]) * factor).astype(BF16)
            stage[j, 1, :, cols] = dot(probs.astype(BF16), g_rows[h]).astype(BF16)
            dq_acc[h] += dot(kv_all[j, 0, :, cols].T, score_grads)

    def backward_row(r):
        pack = pl.ds(r * ny, ny)
        for h, cols in enumerate(head_cols):
            probs = s_scr[pack, h] * (stats[pack, h, 0:1] * finals[h, 0:1])
            score_grads = (probs * (p_scr[pack, h] - finals[h, 1:2])).astype(BF16)
            score_grads = score_grads.reshape(ny * tok, rows)
            probs = probs.astype(BF16).reshape(ny * tok, rows)
            key_grads = (dot(score_grads, q_rows[h]) * factor).astype(BF16)
            stage[pack, 0, :, cols] = key_grads.reshape(ny, tok, HEAD_SIZE)
            value_grads = dot(probs, g_rows[h]).astype(BF16)
            stage[pack, 1, :, cols] = value_grads.reshape(ny, tok, HEAD_SIZE)
            keys = kv_all[pack, 0, :, cols].reshape(ny * tok, HEAD_SIZE)
            dq_acc[h] += dot(keys.T, score_grads)

    def chain(r):
        j = r * ny + y
        live = j != deepest
        for half in range(2):
            total[half] = stage[j, half].astype(F32)
            for dy in range(1, ny):
                yy = (y + dy) % ny

                @pl.when(live & ((r < z) | (y < yy)))
                def _():
                    y_arrival(r, yy, half)
                    total[half] += yrecv[r, yy, half].astype(F32)

            @pl.when(live & (r < z))
            def _():
                stage[j, half] = total[half].astype(BF16)
                z_copy(r, half).start()

    def back_step(r, carry):
        @pl.when(r < z)
        def _():
            backward_row(r)

        for dy in range(1, ny):
            yy = (y + dy) % ny

            @pl.when(y_sends(r, yy))
            def _():
                @pl.when(r == z)
                def _():
                    backward(r * ny + yy)

                for half in range(2):
                    y_copy(r, yy, half).start()

        @pl.when(r == z)
        def _():
            backward(me)

        @pl.when((r > 0) & ((r - 1) * ny + y != deepest))
        def _():
            chain(r - 1)

        return carry

    lax.fori_loop(0, z + 1, back_step, 0)
    cos_t, sin_t = turns[0], turns[1]
    for h in range(kv_local):
        query_grad = dq_acc[h] * factor
        for g in range(group):
            one = query_grad[:, g * tok:(g + 1) * tok]
            a, b = one[:half_head], one[half_head:]
            turned = jnp.concatenate([a * cos_t + b * sin_t, b * cos_t - a * sin_t], axis=0)
            head = (h * group + g) * HEAD_SIZE
            x_t[head:head + HEAD_SIZE, :] = turned.astype(BF16)

    for copy in weights:
        copy.wait()
    def quarter_at(target):
        return pl.ds(pl.multiple_of(target * wide, HEAD_SIZE), wide)

    def query_part(i, carry):
        at = quarter_at(((x + 1 + i // 2) % nx) * 2 + i % 2)
        acc[at] = dot(w_all[at, 0:q_width], x_t[0:q_width])
        return carry

    early = jnp.where(z == nz - 1, 2 * nx - 2, 2 * nx)
    lax.fori_loop(0, early, query_part, 0)
    chain(z)

    def from_above(sz, carry):
        for half in range(2):
            z_arrival(sz, half)
            total[half] += zrecv[sz, half].astype(F32)
        return carry

    lax.fori_loop(z + 1, jnp.where(me == deepest, z + 1, nz), from_above, 0)

    for h, cols in enumerate(head_cols):
        one = total[0, :, cols].T
        a, b = one[:half_head], one[half_head:]
        turned = jnp.concatenate([a * cos_t + b * sin_t, b * cos_t - a * sin_t], axis=0)
        at = q_width + h * HEAD_SIZE
        x_t[at:at + HEAD_SIZE, :] = turned.astype(BF16)
        at = at + kv_width
        x_t[at:at + HEAD_SIZE, :] = total[1, :, cols].T.astype(BF16)

    def key_value_part(target):
        at = quarter_at(target)
        acc[at] += dot(w_all[at, q_width:], x_t[q_width:])

    def piece(target, i):
        return acc[pl.ds(pl.multiple_of(target * wide + i * chunk, HEAD_SIZE), chunk)]

    def sib_copy(tx, i):
        return remote(
            sib_send.at[tx, i], sib_recv.at[tx, i], ss_sem.at[tx, i], sr_sem.at[tx, i],
            me, x * 2 + 1 - core,
        )

    def x_copy(tx, i):
        return remote(
            x_send.at[tx, i], x_recv.at[x, i], xs_sem.at[tx, i], xr_sem.at[x, i],
            me, tx * 2 + core,
        )

    def x_arrival(sx, i):
        remote(
            x_send.at[sx, i], x_recv.at[sx, i], xs_sem.at[sx, i], xr_sem.at[sx, i], me, t
        ).wait_recv()

    def to_sibling(tx):
        key_value_part(tx * 2 + 1 - core)

        def body(i, carry):
            sib_send[tx, i] = piece(tx * 2 + 1 - core, i).astype(BF16)
            sib_copy(tx, i).start()
            return carry

        lax.fori_loop(0, per, body, 0)

    def from_sibling(tx, i):
        part = piece(tx * 2 + core, i)
        sib_copy(tx, i).wait_recv()
        return part + sib_recv[tx, i].astype(F32)

    for dx in range(1, nx):
        tx = (x + dx) % nx
        to_sibling(tx)
        key_value_part(tx * 2 + core)

        def across(i, carry):
            x_send[tx, i] = from_sibling(tx, i).astype(BF16)
            x_copy(tx, i).start()
            return carry

        lax.fori_loop(0, per, across, 0)
    lax.fori_loop(early, 2 * nx, query_part, 0)
    to_sibling(x)
    key_value_part(x * 2 + core)

    def last(i, carry):
        result = from_sibling(x, i)
        for dx in range(1, nx):
            sx = (x + dx) % nx
            x_arrival(sx, i)
            result = result + x_recv[sx, i].astype(F32)
        out_ref[:, pl.ds(pl.multiple_of(i * chunk, chunk), chunk)] = result.T.astype(BF16)
        return carry

    lax.fori_loop(0, per, last, 0)

    for k in range(nz):
        r = z - k
        live = (r >= 0) & (r * ny + y != deepest)
        for half in range(2):
            @pl.when(live & (z < nz - 1))
            def _():
                up_copy(r, half).wait_send()

            for dy in range(1, ny):
                yy = (y + dy) % ny

                @pl.when(live & ((k > 0) | (y < yy)))
                def _():
                    side_copy(r, yy, half).wait_send()
    for r in range(nz):
        for half in range(2):
            for dy in range(1, ny):
                yy = (y + dy) % ny

                @pl.when(y_sends(r, yy))
                def _():
                    y_copy(r, yy, half).wait_send()

            @pl.when((r < z) & (r * ny + y != deepest))
            def _():
                z_copy(r, half).wait_send()

    def drain(i, carry):
        for tx in range(nx):
            sib_copy(tx, i).wait_send()
        for dx in range(1, nx):
            x_copy((x + dx) % nx, i).wait_send()
        return carry

    lax.fori_loop(0, per, drain, 0)


def shards(nz, ny, nx, queries, keys, values, out_grad, ancestry, w_query, key_matrix, value_matrix):
    n = nz * ny
    tok, q_width = queries.shape
    kv_width = keys.shape[1]
    kv_local = kv_width // HEAD_SIZE
    rows = tok * (q_width // kv_width)
    model = w_query.shape[0]
    wide = model // (2 * nx)
    chunk = 256 if wide % 256 == 0 else 128
    per = wide // chunk
    pair = (2, tok, kv_width)
    dma = pltpu.SemaphoreType.DMA
    vmem = pl.BlockSpec(memory_space=pltpu.VMEM)
    hbm = pl.BlockSpec(memory_space=pl.ANY)
    return pl.pallas_call(
        functools.partial(kernel, nz, ny, nx),
        out_shape=jax.ShapeDtypeStruct((tok, wide), BF16),
        in_specs=[pl.BlockSpec(memory_space=pltpu.SMEM)] + [hbm] * 7,
        out_specs=vmem,
        scratch_shapes=[
            pltpu.VMEM((model, q_width + 2 * kv_width), BF16),
            pltpu.VMEM((n,) + pair, BF16),
            pltpu.VMEM((kv_local, rows, HEAD_SIZE), BF16),
            pltpu.VMEM((kv_local, rows, HEAD_SIZE), BF16),
            pltpu.VMEM((n, kv_local, tok, rows), F32),
            pltpu.VMEM((n, kv_local, tok, rows), F32),
            pltpu.VMEM((n, kv_local, 8, rows), F32),
            pltpu.VMEM((kv_local, 8, rows), F32),
            pltpu.VMEM((2, HEAD_SIZE // 2, tok), F32),
            pltpu.VMEM((kv_local, HEAD_SIZE, rows), F32),
            pltpu.VMEM((n,) + pair, BF16),
            pltpu.VMEM((nz, ny) + pair, BF16),
            pltpu.VMEM((nz,) + pair, BF16),
            pltpu.VMEM(pair, F32),
            pltpu.VMEM((q_width + 2 * kv_width, tok), BF16),
            pltpu.VMEM((model, tok), F32),
            pltpu.VMEM((nx, per, chunk, tok), BF16),
            pltpu.VMEM((nx, per, chunk, tok), BF16),
            pltpu.VMEM((nx, per, chunk, tok), BF16),
            pltpu.VMEM((nx, per, chunk, tok), BF16),
            dma((5,)), dma((2, q_width // HEAD_SIZE)), dma((nz, 2)), dma((nz, ny, 2)), dma((n, 2)),
            dma((nz, ny, 2)), dma((nz, ny, 2)), dma((nz, 2)), dma((nz, 2)),
            dma((nx, per)), dma((nx, per)), dma((nx, per)), dma((nx, per)),
        ],
        compiler_params=pltpu.CompilerParams(
            collective_id=0, has_side_effects=True, vmem_limit_bytes=60 * 1024 * 1024
        ),
        name="tree_attention_backward",
    )(ancestry, queries, keys, values, out_grad, w_query, key_matrix, value_matrix)


def solution(mesh):
    n = mesh.shape["ctx"]
    ny = 2 ** ((n.bit_length() - 1) // 2)
    nx = mesh.shape["tp"] // 2
    in_specs = (
        P("ctx", "tp"),
        P("ctx", "tp"),
        P("ctx", "tp"),
        P("ctx", "tp"),
        P(),
        P(None, "tp"),
        P(None, "tp"),
        P(None, "tp"),
    )
    return jax.shard_map(
        functools.partial(shards, n // ny, ny, nx),
        mesh=mesh, in_specs=in_specs, out_specs=P("ctx", "tp"), check_vma=False,
    )
```
